32 devices in a mesh: groups: 2 (over y), ctx: 4 (over z), mp: 2 (over x), sec: 2 (over core).
Axes of the slice: x: 2, y: 2, z: 4, core: 2. Of those that a mesh axis runs over, the one named last changes fastest.
Arguments:
- queries: bfloat16 [1024, 2048], P(('groups', 'ctx'), ('mp', 'sec')), parts along dimension 0, may hold values from -6 to 6
- keys: bfloat16 [1024, 2048], P(('groups', 'ctx'), ('mp', 'sec')), parts along dimension 0, may hold values from -6 to 6
- values: bfloat16 [1024, 2048], P(('groups', 'ctx'), ('mp', 'sec')), parts along dimension 0, may hold values from -6 to 6
- text_keys: bfloat16 [2048, 2048], P('groups', ('mp', 'sec')), parts along dimension 0, may hold values from -6 to 6
- text_values: bfloat16 [2048, 2048], P('groups', ('mp', 'sec')), parts along dimension 0, may hold values from -6 to 6
- segment: int32 [1024], P(('groups', 'ctx')), parts along dimension 0, may hold values from 0 to 3, never falling along the last dimension, each value on 1 to 384 neighbouring positions
- text_len: int32 [8], P('groups'), parts along dimension 0, may hold values from 1 to 256, as said below
- grad_out: bfloat16 [1024, 2048], P(('groups', 'ctx'), ('mp', 'sec')), parts along dimension 0, may hold values from -6 to 6
Outputs:
- output: bfloat16 [1024, 2048], P(('groups', 'ctx'), ('mp', 'sec')), parts along dimension 0
- grad_q: bfloat16 [1024, 2048], P(('groups', 'ctx'), ('mp', 'sec')), parts along dimension 0
- grad_k: bfloat16 [1024, 2048], P(('groups', 'ctx'), ('mp', 'sec')), parts along dimension 0
- grad_v: bfloat16 [1024, 2048], P(('groups', 'ctx'), ('mp', 'sec')), parts along dimension 0
- grad_text_k: float32 [2048, 2048], P('groups', ('mp', 'sec')), parts along dimension 0
- grad_text_v: float32 [2048, 2048], P('groups', ('mp', 'sec')), parts along dimension 0
The draws below stay inside these ranges and needn't reach their ends.
There are 2 independent parts, one for each index of `groups`. The reference program is written for one: setup_inputs(seed, part) draws one part's arguments, and reference() takes and returns one part's arrays. A program takes and returns all parts, laid end to end along the dimension named above; each array names one. Nothing has to cross between parts.
Inputs may be any that keep to these rules, and one draw needn't show every extreme that they name: `segment`: clip numbers never fall along the sequence; each clip holds 1 to 384 latent tokens and one holds exactly 384. `text_len`: one clip in every draw has all 256 text tokens live, the others fewer.
All inputs are finite; a program needn't handle non-finite values.
Results may differ from the reference program's by a relative error of at most 0.0071.
Values may be sent and summed in bfloat16 or wider, within the bound.
No kernel may reach another device: no remote copies, remote signals or barrier semaphores. Data moves between devices by JAX's collectives and lax.ppermute only.
A program may use at most 128 MiB of HBM per device.

```python
import math
import jax
import jax.numpy as jnp
import numpy as np
from jax import lax

HEADS = 16
HD = 128
TXT = 256
CLIPS = 4
SEQ = 512
SEG_MOST = 384


def draw_text_len(key, part):
    key_lengths, key_chosen = jax.random.split(key)
    lengths = jax.random.randint(key_lengths, (CLIPS,), 1, TXT, dtype=jnp.int32)
    chosen = jax.random.randint(key_chosen, (), 0, CLIPS, dtype=jnp.int32)
    return jnp.where(jnp.arange(CLIPS, dtype=jnp.int32) == chosen, TXT, lengths).astype(jnp.int32)


def shard_levels(stream_key, shape, cuts, low, largest):
    def one(dim, shards_of):
        heights = jax.random.uniform(jax.random.fold_in(jax.random.fold_in(stream_key, 6), dim), (shards_of,), jnp.float32, low / len(cuts), largest / len(cuts))
        return jnp.repeat(jnp.exp(heights), shape[dim] // shards_of).reshape((-1,) + (1,) * (len(shape) - dim - 1))

    gain = one(*cuts[0])
    for cut in cuts[1:]:
        gain = gain * one(*cut)
    return gain


def length_profile(amount, total, reach, lean):
    weights = [(1 << 20) // math.isqrt(rank ** lean) + 1 for rank in range(2, amount + 1)]
    spare, given = total - reach - (amount - 1), [1] * (amount - 1)
    while spare > 0:
        movable = [i for i in range(amount - 1) if given[i] < reach]
        whole, remaining = sum([weights[i] for i in movable]), spare
        for i in movable:
            more = min(reach - given[i], max(1, remaining * weights[i] // whole), spare)
            given[i] = given[i] + more
            spare = spare - more
    return np.array([reach] + given)


def ragged_sizes(own_key, number_of, total, bound, lean):
    if number_of == 2:
        one = jax.random.randint(own_key, (), max(1, total - bound), min(bound, total - 1) + 1)
        return jnp.stack([one, total - one])
    tallies = jnp.asarray(length_profile(number_of, total, bound, lean), jnp.int32)
    twos = (number_of - 1) // 2
    donor, taker = tallies[1:1 + 2 * twos:2], tallies[2:2 + 2 * twos:2]
    room = jnp.minimum(donor - 1, bound - taker)
    shifted = jax.random.randint(jax.random.fold_in(own_key, 1), (twos,), 0, 1 << 20) % (room + 1)
    tallies = tallies.at[1:1 + 2 * twos:2].set(donor - shifted).at[2:2 + 2 * twos:2].set(taker + shifted)
    return tallies[jax.random.permutation(jax.random.fold_in(own_key, 2), number_of)]


def centred(key, shape, width, bound, pieces=(), held_as=jnp.bfloat16):
    array = jax.random.normal(key, shape, jnp.float32) * width
    if len(pieces) > 0:
        array = shard_levels(key, shape, pieces, -0.22, 0.18) * array
    return jnp.clip(array, min=-bound, max=bound).astype(held_as)


def setup_inputs(seed: int = 0, part: int = 0) -> dict:
    streams_of = jax.random.split(jax.random.key(seed), 9)
    part_keys = jax.random.split(jax.random.fold_in(streams_of[8], part), 9)
    queries = centred(part_keys[0], (SEQ, HEADS * HD), 1.0, 6.0, ((0, 4), (1, 4)))
    keys = centred(part_keys[1], (SEQ, HEADS * HD), 1.0, 6.0, ((0, 4), (1, 4)))
    values = centred(part_keys[2], (SEQ, HEADS * HD), 1.0, 6.0, ((0, 4), (1, 4)))
    text_keys = centred(part_keys[3], (CLIPS * TXT, HEADS * HD), 1.0, 6.0, ((1, 4),))
    text_values = centred(part_keys[4], (CLIPS * TXT, HEADS * HD), 1.0, 6.0, ((1, 4),))
    segment = jnp.searchsorted(jnp.cumsum(ragged_sizes(part_keys[5], CLIPS, SEQ, SEG_MOST, 1)), jnp.arange(SEQ), side="right").astype(jnp.int32)
    text_len = draw_text_len(jax.random.fold_in(jax.random.fold_in(streams_of[8], part), 71), part)
    grad_out = centred(part_keys[7], (SEQ, HEADS * HD), 1.0, 6.0, ((0, 4), (1, 4)))
    return dict(queries=queries, keys=keys, values=values, text_keys=text_keys, text_values=text_values, segment=segment, text_len=text_len, grad_out=grad_out)


epsilon = 1e-06

def rms_norm(matrix):
    return matrix * lax.rsqrt(lax.optimization_barrier(jnp.mean(matrix * matrix, axis=-1, keepdims=True)) + epsilon)

def rms_back(matrix, upstream):
    inverse = lax.rsqrt(lax.optimization_barrier(jnp.mean(matrix * matrix, axis=-1, keepdims=True)) + epsilon)
    inner = lax.optimization_barrier(jnp.sum(upstream * matrix, axis=-1, keepdims=True)) / matrix.shape[-1]
    return upstream * inverse - matrix * inner * inverse * inverse * inverse

def split_heads(matrix):
    return jnp.transpose(matrix.reshape(matrix.shape[0], HEADS, HD), (1, 0, 2))

def join_heads(stacked):
    return jnp.transpose(stacked, (1, 0, 2)).reshape(stacked.shape[1], -1)

def reference(queries, keys, values, text_keys, text_values, segment, text_len, grad_out):
    score_scale = 1.0 / math.sqrt(HD)
    length = queries.shape[0]
    text_rows = text_keys.shape[0]
    position = jnp.arange(text_rows, dtype=jnp.int32)
    text_clip = (position // TXT).astype(jnp.int32)
    text_limit = text_len[text_clip]
    text_mask = (segment[:, None] == text_clip[None, :]) & (position % TXT < text_limit)[None, :]
    allowed = jnp.concatenate([segment[:, None] == segment[None, :], text_mask], axis=1)

    def one_head(inputs):
        query_h, key_h, value_h, text_kh, text_vh, grad_h = inputs
        query_f = query_h.astype(jnp.float32)
        key_f = key_h.astype(jnp.float32)
        text_f = text_kh.astype(jnp.float32)
        query_n = rms_norm(query_f).astype(jnp.bfloat16)
        key_all = jnp.concatenate([rms_norm(key_f).astype(jnp.bfloat16), rms_norm(text_f).astype(jnp.bfloat16)], axis=0)
        value_all = jnp.concatenate([value_h, text_vh], axis=0)
        logits = jnp.dot(query_n, key_all.T, preferred_element_type=jnp.float32) * score_scale
        expon = jnp.where(allowed, jnp.exp(logits), 0.0)
        weight_bf = expon.astype(jnp.bfloat16)
        norm_sum = lax.optimization_barrier(jnp.sum(weight_bf.astype(jnp.float32), axis=1))
        attended = (jnp.dot(weight_bf, value_all, preferred_element_type=jnp.float32) / norm_sum[:, None]).astype(jnp.bfloat16)
        probs = expon / norm_sum[:, None]
        weights = probs.astype(jnp.bfloat16)
        dvalue = jnp.dot(weights.T, grad_h, preferred_element_type=jnp.float32)
        dprob = jnp.dot(grad_h, value_all.T, preferred_element_type=jnp.float32)
        inner = lax.optimization_barrier(jnp.sum(grad_h.astype(jnp.float32) * attended.astype(jnp.float32), axis=1))
        dscore = (probs * (dprob - inner[:, None])).astype(jnp.bfloat16)
        dquery = jnp.dot(dscore, key_all, preferred_element_type=jnp.float32) * score_scale
        dkey = jnp.dot(dscore.T, query_n, preferred_element_type=jnp.float32) * score_scale
        return (attended, rms_back(query_f, dquery).astype(jnp.bfloat16), rms_back(key_f, dkey[:length]).astype(jnp.bfloat16), dvalue[:length].astype(jnp.bfloat16), rms_back(text_f, dkey[length:]), dvalue[length:])
    results = lax.map(one_head, (split_heads(queries), split_heads(keys), split_heads(values), split_heads(text_keys), split_heads(text_values), split_heads(grad_out)))
    return (join_heads(results[0]), join_heads(results[1]), join_heads(results[2]), join_heads(results[3]), join_heads(results[4]), join_heads(results[5]))
```

```python
import functools
import math

import jax
import jax.numpy as jnp
from jax import lax
from jax.experimental import pallas as pl
from jax.experimental.pallas import tpu as pltpu
from jax.sharding import PartitionSpec as P

HD = 128
SEG_ROWS = 16
FAR = 16384.0
KEY_BLOCK = 256
ROW_BLOCK = 512

epsilon = 1e-06

F32 = jnp.float32
BF16 = jnp.bfloat16


def inverse_rms(x):
    return lax.rsqrt(jnp.mean(x * x, axis=-1, keepdims=True) + epsilon)


def norm_back(x, upstream):
    inverse = inverse_rms(x)
    inner = jnp.sum(upstream * x, axis=-1, keepdims=True) * (1.0 / HD)
    return upstream * inverse - x * (inner * inverse * inverse * inverse)


def dot(a, b, contract):
    return lax.dot_general(a, b, ((contract[:1], contract[1:]), ((), ())), preferred_element_type=F32)


def pack_kernel(chunks, q_ref, k_ref, v_ref, g_ref, seg_ref, *outs):
    length = q_ref.shape[0]
    for (first, count), out in zip(chunks, outs):
        for b in range(count):
            cols = pl.ds((first + b) * HD, HD)
            for a, ref in enumerate((q_ref, k_ref)):
                x = ref[:, cols].astype(F32)
                out[pl.ds((4 * b + a) * length, length), :] = (x * inverse_rms(x)).astype(BF16)
            for a, ref in enumerate((v_ref, g_ref)):
                out[pl.ds((4 * b + 2 + a) * length, length), :] = ref[:, cols]
        seg = seg_ref[...].astype(F32).astype(BF16)
        out[pl.ds(4 * count * length, SEG_ROWS), :] = jnp.broadcast_to(seg, (SEG_ROWS, length))


def pack(queries, keys, values, grad_out, segment, chunks):
    length = queries.shape[0]
    return pl.pallas_call(
        functools.partial(pack_kernel, chunks),
        out_shape=[
            jax.ShapeDtypeStruct((4 * count * length + SEG_ROWS, HD), BF16) for _, count in chunks
        ],
        name="pack",
    )(queries, keys, values, grad_out, segment.reshape(1, length))


def attend_kernel(n, length, count, routed, *refs):
    refs = list(refs)
    len_ref = refs.pop(0)
    pieces = [refs.pop(0) for _ in range(6 if routed else 2)]
    q_raw, k_raw, tk_ref, tv_ref = refs[:4]
    out_ref, gq_ref, gk_ref, gv_ref, gtk_ref, gtv_ref = refs[-18:-12]
    held, qx, kx, vx, gx, e_ref, dp_ref, dk_ref, dv_ref, dq_ref, att_ref, sems = refs[-12:]
    text_rows = tk_ref.shape[0]
    clips = len_ref.shape[0]
    per_clip = text_rows // clips
    video = n * length
    total = video + text_rows
    head = pl.program_id(0)
    rows_of = min(video, ROW_BLOCK)
    row_blocks = video // rows_of
    scale = 1.0 / math.sqrt(HD)
    exponent = scale * math.log2(math.e)
    seg_at = 4 * count * length

    @pl.when(head == 0)
    def _():
        me = lax.axis_index("ctx")
        if routed:
            own, near, far, hop_far, hop_near, last = pieces
            end = (me == 0) | (me == 3)

            def copy(source, slot):
                return pltpu.make_async_copy(source, held.at[slot], sems.at[slot])

            copy(own, 0).start()
            copy(near, 1).start()

            @pl.when(end)
            def _():
                copy(hop_far, 2).start()
                copy(last, 3).start()

            @pl.when(jnp.logical_not(end))
            def _():
                copy(hop_near, 2).start()
                copy(far, 3).start()

            for slot in range(4):
                copy(own, slot).wait()
        else:
            own, gathered = pieces

            def fetch(s, _):
                source = lax.rem(me + s, n)
                pltpu.make_async_copy(gathered.at[source], held.at[s], sems.at[0]).start()
                pltpu.make_async_copy(gathered.at[source], held.at[s], sems.at[0]).wait()
                return 0

            lax.fori_loop(0, n, fetch, 0)

        lane = lax.broadcasted_iota(jnp.int32, (length, HD), 1)
        sub = lax.broadcasted_iota(jnp.int32, (HD, length), 0).astype(F32)

        def mask_rows(s, _):
            seg = held[s, pl.ds(seg_at, SEG_ROWS), :].astype(F32)[0:1, :]
            onehot = jnp.where(jnp.broadcast_to(seg, (HD, length)) == sub, 1.0, 0.0).T
            rows = pl.ds(pl.multiple_of(s * length, length), length)
            qx[rows, HD:] = jnp.where(lane == clips, 1.0, onehot).astype(BF16)
            kx[rows, HD:] = jnp.where(lane < clips, (onehot - 1.0) * FAR, 0.0).astype(BF16)
            return 0

        lax.fori_loop(0, n, mask_rows, 0, unroll=n <= 4)
        lane = lax.broadcasted_iota(jnp.int32, (per_clip, HD), 1)
        place = lax.broadcasted_iota(jnp.int32, (per_clip, HD), 0)
        for c in range(clips):
            other = jnp.where((lane < clips) & (lane != c), -FAR, 0.0)
            dead = jnp.where((lane == clips) & (place >= len_ref[c]), -FAR, 0.0)
            kx[pl.ds(video + c * per_clip, per_clip), HD:] = (other + dead).astype(BF16)

    def place_rows(s, _):
        rows = pl.ds(pl.multiple_of(s * length, length), length)
        for a, (ref, cols) in enumerate(((qx, pl.ds(0, HD)), (kx, pl.ds(0, HD)), (vx, pl.ds(0, HD)), (gx, pl.ds(0, HD)))):
            at = pl.multiple_of((4 * head + a) * length, length)
            ref[rows, cols] = held[s, pl.ds(at, length), :]
        return 0

    lax.fori_loop(0, n, place_rows, 0, unroll=n <= 4)
    text = tk_ref[...].astype(F32)
    kx[pl.ds(video, text_rows), :HD] = (text * inverse_rms(text)).astype(BF16)
    vx[pl.ds(video, text_rows), :] = tv_ref[...]

    def rows_step(rb, first):
        rows = pl.ds(pl.multiple_of(rb * rows_of, rows_of), rows_of)
        q_all = qx[rows, :]
        q_here = qx[rows, :HD]
        g_here = gx[rows, :]

        def score(kb, sums):
            at = pl.ds(pl.multiple_of(kb * KEY_BLOCK, KEY_BLOCK), KEY_BLOCK)
            e = jnp.exp2(dot(kx[at, :], q_all, (1, 1)) * exponent)
            dp = dot(vx[at, :], g_here, (1, 1))
            e_ref[at, :] = e
            dp_ref[at, :] = dp
            shape = (KEY_BLOCK // 8, 8, rows_of)
            return (
                sums[0] + jnp.sum(e.reshape(shape), axis=0),
                sums[1] + jnp.sum((e * dp).reshape(shape), axis=0),
            )

        blocks = total // KEY_BLOCK
        zero = jnp.zeros((8, rows_of), F32)
        sums = lax.fori_loop(0, blocks, score, (zero, zero), unroll=blocks <= 8)
        inv = 1.0 / jnp.sum(sums[0], axis=0, keepdims=True)
        inner = jnp.sum(sums[1], axis=0, keepdims=True) * inv

        def add(ref, at, value):
            if row_blocks == 1:
                ref[at, :] = value
            else:
                ref[at, :] = jnp.where(rb == 0, value, ref[at, :] + value)

        def terms(at, cols):
            p = e_ref[at, cols] * inv[:, cols]
            ds = p * (dp_ref[at, cols] - inner[:, cols])
            return p.astype(BF16), ds.astype(BF16)

        everything = slice(0, rows_of)
        mine = slice(0, length)

        def query_side(at, p, ds, start):
            att = dot(p, vx[at, :], (0, 0))
            dq = dot(ds, kx[at, :HD], (0, 0))
            if start:
                att_ref[...] = att
                dq_ref[...] = dq
            else:
                att_ref[...] += att
                dq_ref[...] += dq

        def own_rows(at, p, ds, start=False):
            if row_blocks == 1:
                query_side(at, p[:, mine], ds[:, mine], start)
            else:

                @pl.when(rb == 0)
                def _():
                    query_side(at, p[:, mine], ds[:, mine], start)

        own = pl.ds(0, length)
        p, ds = terms(own, everything)
        add(dk_ref, own, dot(ds, q_here, (1, 0)))
        add(dv_ref, own, dot(p, g_here, (1, 0)))
        own_rows(own, p, ds, True)

        def others():
            def other(s, _):
                at = pl.ds(pl.multiple_of(s * length, length), length)
                p, ds = terms(at, mine)
                query_side(at, p, ds, False)
                return 0

            lax.fori_loop(1, n, other, 0, unroll=n <= 4)

        if row_blocks == 1:
            others()
        else:
            pl.when(rb == 0)(others)
        for c in range(text_rows // KEY_BLOCK):
            at = pl.ds(video + c * KEY_BLOCK, KEY_BLOCK)
            to = pl.ds(c * KEY_BLOCK, KEY_BLOCK)
            p, ds = terms(at, everything)
            add(gtk_ref, to, dot(ds, q_here, (1, 0)))
            add(gtv_ref, to, dot(p, g_here, (1, 0)))
            own_rows(at, p, ds)

    if row_blocks == 1:
        rows_step(0, True)
    else:

        def step(rb, _):
            rows_step(rb, False)
            return 0

        lax.fori_loop(0, row_blocks, step, 0)

    out_ref[...] = att_ref[...].astype(BF16)
    gq_ref[...] = norm_back(q_raw[...].astype(F32), dq_ref[...] * scale).astype(BF16)
    gk_ref[...] = norm_back(k_raw[...].astype(F32), dk_ref[...] * scale).astype(BF16)
    gv_ref[...] = dv_ref[...].astype(BF16)
    gtk_ref[...] = norm_back(tk_ref[...].astype(F32), gtk_ref[...] * scale)


def attend(n, chunk, text_len, pieces, queries, keys, text_keys, text_values, before):
    first, count = chunk
    routed = len(pieces) > 2
    length, width = queries.shape
    text_rows = text_keys.shape[0]
    video = n * length
    total = video + text_rows
    rows_of = min(video, ROW_BLOCK)
    anywhere = pl.BlockSpec(memory_space=pl.ANY)

    def column(rows):
        return pl.BlockSpec((rows, HD), lambda h: (0, first + h))

    in_specs = (
        [pl.BlockSpec(memory_space=pltpu.SMEM)]
        + [anywhere] * len(pieces)
        + [column(length)] * 2
        + [column(text_rows)] * 2
        + [anywhere] * len(before)
    )
    out_rows = [length] * 4 + [text_rows] * 2
    out_types = [BF16] * 4 + [F32] * 2
    operands = [text_len, *pieces, queries, keys, text_keys, text_values, *before]
    base = len(operands) - len(before)
    pairs = count * total * rows_of * (video // rows_of)
    return pl.pallas_call(
        functools.partial(attend_kernel, n, length, count, routed),
        grid=(count,),
        in_specs=in_specs,
        out_specs=[column(rows) for rows in out_rows],
        out_shape=[
            jax.ShapeDtypeStruct((rows, width), dtype) for rows, dtype in zip(out_rows, out_types)
        ],
        scratch_shapes=[
            pltpu.VMEM((n, 4 * count * length + SEG_ROWS, HD), BF16),
            pltpu.VMEM((video, 2 * HD), BF16),
            pltpu.VMEM((total, 2 * HD), BF16),
            pltpu.VMEM((total, HD), BF16),
            pltpu.VMEM((video, HD), BF16),
            pltpu.VMEM((total, rows_of), F32),
            pltpu.VMEM((total, rows_of), F32),
            pltpu.VMEM((length, HD), F32),
            pltpu.VMEM((length, HD), F32),
            pltpu.VMEM((length, HD), F32),
            pltpu.VMEM((length, HD), F32),
            pltpu.SemaphoreType.DMA((4,)),
        ],
        input_output_aliases={base + i: i for i in range(len(before))},
        compiler_params=pltpu.CompilerParams(vmem_limit_bytes=56 * 1024 * 1024),
        cost_estimate=pl.CostEstimate(
            flops=12 * pairs * HD, bytes_accessed=count * 3 * 1024 * 1024, transcendentals=pairs
        ),
        name="attend",
    )(*operands)


def shards(n, queries, keys, values, text_keys, text_values, segment, text_len, grad_out):
    heads = queries.shape[1] // HD
    half = max(heads // 2, 1)
    chunks = [(first, half) for first in range(0, heads, half)]
    payloads = pack(queries, keys, values, grad_out, segment, chunks)

    def send(x, pairs):
        return lax.ppermute(x, "ctx", pairs)

    if n == 4:
        outer = [(0, 1), (1, 0), (2, 3), (3, 2)]
        middle = [(1, 2), (2, 1)]
        outward = [(1, 0), (2, 3)]
        first = [(send(x, outer), send(x, middle)) for x in payloads]
        pieces = []
        for x, (near, far) in zip(payloads, first):
            hop_far = send(far, outward)
            hop_near = send(near, middle)
            last = send(hop_near, outward)
            pieces.append((x, near, far, hop_far, hop_near, last))
    else:
        pieces = [(x, lax.all_gather(x, "ctx", axis=0)) for x in payloads]
    outs = ()
    for chunk, piece in zip(chunks, pieces):
        outs = attend(n, chunk, text_len, piece, queries, keys, text_keys, text_values, outs)
    return tuple(outs)


def solution(mesh):
    rows = P(("groups", "ctx"), ("mp", "sec"))
    text = P("groups", ("mp", "sec"))
    in_specs = (rows, rows, rows, text, text, P(("groups", "ctx")), P("groups"), rows)
    out_specs = (rows, rows, rows, rows, text, text)
    return jax.shard_map(
        functools.partial(shards, mesh.shape["ctx"]),
        mesh=mesh,
        in_specs=in_specs,
        out_specs=out_specs,
        check_vma=False,
    )
```

```python
import functools
import math

import jax
import jax.numpy as jnp
from jax import lax
from jax.experimental import pallas as pl
from jax.experimental.pallas import tpu as pltpu
from jax.sharding import PartitionSpec as P

HD = 128
SEG_ROWS = 16
FAR = 16384.0
KEY_BLOCK = 256
ROW_BLOCK = 512

epsilon = 1e-06

F32 = jnp.float32
BF16 = jnp.bfloat16


def inverse_rms(x):
    return lax.rsqrt(jnp.mean(x * x, axis=-1, keepdims=True) + epsilon)


def norm_back(x, upstream):
    inverse = inverse_rms(x)
    inner = jnp.sum(upstream * x, axis=-1, keepdims=True) * (1.0 / HD)
    return upstream * inverse - x * (inner * inverse * inverse * inverse)


def dot(a, b, contract):
    return lax.dot_general(a, b, ((contract[:1], contract[1:]), ((), ())), preferred_element_type=F32)


def pack_kernel(chunks, q_ref, k_ref, v_ref, g_ref, seg_ref, *outs):
    length = q_ref.shape[0]
    for (first, count), out in zip(chunks, outs):
        for b in range(count):
            cols = pl.ds((first + b) * HD, HD)
            for a, ref in enumerate((q_ref, k_ref)):
                x = ref[:, cols].astype(F32)
                out[pl.ds((4 * b + a) * length, length), :] = (x * inverse_rms(x)).astype(BF16)
            for a, ref in enumerate((v_ref, g_ref)):
                out[pl.ds((4 * b + 2 + a) * length, length), :] = ref[:, cols]
        seg = seg_ref[...].astype(F32).astype(BF16)
        out[pl.ds(4 * count * length, SEG_ROWS), :] = jnp.broadcast_to(seg, (SEG_ROWS, length))


def pack(queries, keys, values, grad_out, segment, chunks):
    length = queries.shape[0]
    return pl.pallas_call(
        functools.partial(pack_kernel, chunks),
        out_shape=[
            jax.ShapeDtypeStruct((4 * count * length + SEG_ROWS, HD), BF16) for _, count in chunks
        ],
        name="pack",
    )(queries, keys, values, grad_out, segment.reshape(1, length))


def attend_kernel(n, length, count, routed, *refs):
    refs = list(refs)
    len_ref = refs.pop(0)
    pieces = [refs.pop(0) for _ in range(5 if routed else 2)]
    q_raw, k_raw, tk_ref, tv_ref = refs[:4]
    out_ref, gq_ref, gk_ref, gv_ref, gtk_ref, gtv_ref = refs[-18:-12]
    held, qx, kx, vx, gx, e_ref, dp_ref, dk_ref, dv_ref, dq_ref, att_ref, sems = refs[-12:]
    text_rows = tk_ref.shape[0]
    clips = len_ref.shape[0]
    per_clip = text_rows // clips
    video = n * length
    total = video + text_rows
    head = pl.program_id(0)
    rows_of = min(video, ROW_BLOCK)
    row_blocks = video // rows_of
    scale = 1.0 / math.sqrt(HD)
    exponent = scale * math.log2(math.e)
    seg_at = 4 * count * length

    @pl.when(head == 0)
    def _():
        me = lax.axis_index("ctx")
        if routed:
            own, near, skip, far, last = pieces
            end = (me == 0) | (me == 3)

            def copy(source, slot):
                return pltpu.make_async_copy(source, held.at[slot], sems.at[slot])

            copy(own, 0).start()
            copy(near, 1).start()
            copy(skip, 2).start()

            @pl.when(end)
            def _():
                copy(last, 3).start()

            @pl.when(jnp.logical_not(end))
            def _():
                copy(far, 3).start()

            for slot in range(4):
                copy(own, slot).wait()
        else:
            own, gathered = pieces

            def fetch(s, _):
                source = lax.rem(me + s, n)
                pltpu.make_async_copy(gathered.at[source], held.at[s], sems.at[0]).start()
                pltpu.make_async_copy(gathered.at[source], held.at[s], sems.at[0]).wait()
                return 0

            lax.fori_loop(0, n, fetch, 0)

        lane = lax.broadcasted_iota(jnp.int32, (length, HD), 1)
        sub = lax.broadcasted_iota(jnp.int32, (HD, length), 0).astype(F32)

        def mask_rows(s, _):
            seg = held[s, pl.ds(seg_at, SEG_ROWS), :].astype(F32)[0:1, :]
            onehot = jnp.where(jnp.broadcast_to(seg, (HD, length)) == sub, 1.0, 0.0).T
            rows = pl.ds(pl.multiple_of(s * length, length), length)
            qx[rows, HD:] = jnp.where(lane == clips, 1.0, onehot).astype(BF16)
            kx[rows, HD:] = jnp.where(lane < clips, (onehot - 1.0) * FAR, 0.0).astype(BF16)
            return 0

        lax.fori_loop(0, n, mask_rows, 0, unroll=n <= 4)
        lane = lax.broadcasted_iota(jnp.int32, (per_clip, HD), 1)
        place = lax.broadcasted_iota(jnp.int32, (per_clip, HD), 0)
        for c in range(clips):
            other = jnp.where((lane < clips) & (lane != c), -FAR, 0.0)
            dead = jnp.where((lane == clips) & (place >= len_ref[c]), -FAR, 0.0)
            kx[pl.ds(video + c * per_clip, per_clip), HD:] = (other + dead).astype(BF16)

    def place_rows(s, _):
        rows = pl.ds(pl.multiple_of(s * length, length), length)
        for a, (ref, cols) in enumerate(((qx, pl.ds(0, HD)), (kx, pl.ds(0, HD)), (vx, pl.ds(0, HD)), (gx, pl.ds(0, HD)))):
            at = pl.multiple_of((4 * head + a) * length, length)
            ref[rows, cols] = held[s, pl.ds(at, length), :]
        return 0

    lax.fori_loop(0, n, place_rows, 0, unroll=n <= 4)
    text = tk_ref[...].astype(F32)
    kx[pl.ds(video, text_rows), :HD] = (text * inverse_rms(text)).astype(BF16)
    vx[pl.ds(video, text_rows), :] = tv_ref[...]

    def rows_step(rb, first):
        rows = pl.ds(pl.multiple_of(rb * rows_of, rows_of), rows_of)
        q_all = qx[rows, :]
        q_here = qx[rows, :HD]
        g_here = gx[rows, :]

        def score(kb, sums):
            at = pl.ds(pl.multiple_of(kb * KEY_BLOCK, KEY_BLOCK), KEY_BLOCK)
            e = jnp.exp2(dot(kx[at, :], q_all, (1, 1)) * exponent)
            dp = dot(vx[at, :], g_here, (1, 1))
            e_ref[at, :] = e
            dp_ref[at, :] = dp
            shape = (KEY_BLOCK // 8, 8, rows_of)
            return (
                sums[0] + jnp.sum(e.reshape(shape), axis=0),
                sums[1] + jnp.sum((e * dp).reshape(shape), axis=0),
            )

        blocks = total // KEY_BLOCK
        zero = jnp.zeros((8, rows_of), F32)
        sums = lax.fori_loop(0, blocks, score, (zero, zero), unroll=blocks <= 8)
        inv = 1.0 / jnp.sum(sums[0], axis=0, keepdims=True)
        inner = jnp.sum(sums[1], axis=0, keepdims=True) * inv

        def add(ref, at, value):
            if row_blocks == 1:
                ref[at, :] = value
            else:
                ref[at, :] = jnp.where(rb == 0, value, ref[at, :] + value)

        def terms(at, cols):
            p = e_ref[at, cols] * inv[:, cols]
            ds = p * (dp_ref[at, cols] - inner[:, cols])
            return p.astype(BF16), ds.astype(BF16)

        everything = slice(0, rows_of)
        mine = slice(0, length)

        def query_side(at, p, ds, start):
            att = dot(p, vx[at, :], (0, 0))
            dq = dot(ds, kx[at, :HD], (0, 0))
            if start:
                att_ref[...] = att
                dq_ref[...] = dq
            else:
                att_ref[...] += att
                dq_ref[...] += dq

        def own_rows(at, p, ds, start=False):
            if row_blocks == 1:
                query_side(at, p[:, mine], ds[:, mine], start)
            else:

                @pl.when(rb == 0)
                def _():
                    query_side(at, p[:, mine], ds[:, mine], start)

        own = pl.ds(0, length)
        p, ds = terms(own, everything)
        add(dk_ref, own, dot(ds, q_here, (1, 0)))
        add(dv_ref, own, dot(p, g_here, (1, 0)))
        own_rows(own, p, ds, True)

        def others():
            def other(s, _):
                at = pl.ds(pl.multiple_of(s * length, length), length)
                p, ds = terms(at, mine)
                query_side(at, p, ds, False)
                return 0

            lax.fori_loop(1, n, other, 0, unroll=n <= 4)

        if row_blocks == 1:
            others()
        else:
            pl.when(rb == 0)(others)
        for c in range(text_rows // KEY_BLOCK):
            at = pl.ds(video + c * KEY_BLOCK, KEY_BLOCK)
            to = pl.ds(c * KEY_BLOCK, KEY_BLOCK)
            p, ds = terms(at, everything)
            add(gtk_ref, to, dot(ds, q_here, (1, 0)))
            add(gtv_ref, to, dot(p, g_here, (1, 0)))
            own_rows(at, p, ds)

    if row_blocks == 1:
        rows_step(0, True)
    else:

        def step(rb, _):
            rows_step(rb, False)
            return 0

        lax.fori_loop(0, row_blocks, step, 0)

    out_ref[...] = att_ref[...].astype(BF16)
    gq_ref[...] = norm_back(q_raw[...].astype(F32), dq_ref[...] * scale).astype(BF16)
    gk_ref[...] = norm_back(k_raw[...].astype(F32), dk_ref[...] * scale).astype(BF16)
    gv_ref[...] = dv_ref[...].astype(BF16)
    gtk_ref[...] = norm_back(tk_ref[...].astype(F32), gtk_ref[...] * scale)


def attend(n, chunk, text_len, pieces, queries, keys, text_keys, text_values, before):
    first, count = chunk
    routed = len(pieces) > 2
    length, width = queries.shape
    text_rows = text_keys.shape[0]
    video = n * length
    total = video + text_rows
    rows_of = min(video, ROW_BLOCK)
    anywhere = pl.BlockSpec(memory_space=pl.ANY)

    def column(rows):
        return pl.BlockSpec((rows, HD), lambda h: (0, first + h))

    in_specs = (
        [pl.BlockSpec(memory_space=pltpu.SMEM)]
        + [anywhere] * len(pieces)
        + [column(length)] * 2
        + [column(text_rows)] * 2
        + [anywhere] * len(before)
    )
    out_rows = [length] * 4 + [text_rows] * 2
    out_types = [BF16] * 4 + [F32] * 2
    operands = [text_len, *pieces, queries, keys, text_keys, text_values, *before]
    base = len(operands) - len(before)
    pairs = count * total * rows_of * (video // rows_of)
    return pl.pallas_call(
        functools.partial(attend_kernel, n, length, count, routed),
        grid=(count,),
        in_specs=in_specs,
        out_specs=[column(rows) for rows in out_rows],
        out_shape=[
            jax.ShapeDtypeStruct((rows, width), dtype) for rows, dtype in zip(out_rows, out_types)
        ],
        scratch_shapes=[
            pltpu.VMEM((n, 4 * count * length + SEG_ROWS, HD), BF16),
            pltpu.VMEM((video, 2 * HD), BF16),
            pltpu.VMEM((total, 2 * HD), BF16),
            pltpu.VMEM((total, HD), BF16),
            pltpu.VMEM((video, HD), BF16),
            pltpu.VMEM((total, rows_of), F32),
            pltpu.VMEM((total, rows_of), F32),
            pltpu.VMEM((length, HD), F32),
            pltpu.VMEM((length, HD), F32),
            pltpu.VMEM((length, HD), F32),
            pltpu.VMEM((length, HD), F32),
            pltpu.SemaphoreType.DMA((4,)),
        ],
        input_output_aliases={base + i: i for i in range(len(before))},
        compiler_params=pltpu.CompilerParams(vmem_limit_bytes=(16 if routed else 56) * 1024 * 1024),
        cost_estimate=pl.CostEstimate(
            flops=12 * pairs * HD, bytes_accessed=count * 3 * 1024 * 1024, transcendentals=pairs
        ),
        name="attend",
    )(*operands)


def shards(n, queries, keys, values, text_keys, text_values, segment, text_len, grad_out):
    heads = queries.shape[1] // HD
    half = max(heads // 2, 1)
    chunks = [(first, half) for first in range(0, heads, half)]
    payloads = pack(queries, keys, values, grad_out, segment, chunks)

    def send(x, pairs):
        return lax.ppermute(x, "ctx", pairs)

    if n == 4:
        outer = [(0, 1), (1, 0), (2, 3), (3, 2)]
        across = [(0, 2), (2, 0), (1, 3), (3, 1)]
        middle = [(1, 2), (2, 1)]
        outward = [(1, 0), (2, 3)]
        pieces = []
        for x in payloads:
            skip = send(x, across)
            near = send(x, outer)
            far = send(x, middle)
            last = send(skip, outward)
            pieces.append((x, near, skip, far, last))
    else:
        pieces = [(x, lax.all_gather(x, "ctx", axis=0)) for x in payloads]
    outs = ()
    for chunk, piece in zip(chunks, pieces):
        outs = attend(n, chunk, text_len, piece, queries, keys, text_keys, text_values, outs)
    return tuple(outs)


def solution(mesh):
    rows = P(("groups", "ctx"), ("mp", "sec"))
    text = P("groups", ("mp", "sec"))
    in_specs = (rows, rows, rows, text, text, P(("groups", "ctx")), P("groups"), rows)
    out_specs = (rows, rows, rows, rows, text, text)
    return jax.shard_map(
        functools.partial(shards, mesh.shape["ctx"]),
        mesh=mesh,
        in_specs=in_specs,
        out_specs=out_specs,
        check_vma=False,
    )
```

```python
import functools
import math

import jax
import jax.numpy as jnp
from jax import lax
from jax.experimental import pallas as pl
from jax.experimental.pallas import tpu as pltpu
from jax.sharding import PartitionSpec as P

HD = 128
SEG_ROWS = 16
FAR = 16384.0
KEY_BLOCK = 256
ROW_BLOCK = 512

epsilon = 1e-06

F32 = jnp.float32
BF16 = jnp.bfloat16


def inverse_rms(x):
    return lax.rsqrt(jnp.mean(x * x, axis=-1, keepdims=True) + epsilon)


def norm_back(x, upstream):
    inverse = inverse_rms(x)
    inner = jnp.sum(upstream * x, axis=-1, keepdims=True) * (1.0 / HD)
    return upstream * inverse - x * (inner * inverse * inverse * inverse)


def dot(a, b, contract):
    return lax.dot_general(a, b, ((contract[:1], contract[1:]), ((), ())), preferred_element_type=F32)


def pack_kernel(chunks, q_ref, k_ref, v_ref, g_ref, seg_ref, *outs):
    length = q_ref.shape[0]
    for (first, count), out in zip(chunks, outs):
        for b in range(count):
            cols = pl.ds((first + b) * HD, HD)
            for a, ref in enumerate((q_ref, k_ref)):
                x = ref[:, cols].astype(F32)
                out[pl.ds((4 * b + a) * length, length), :] = (x * inverse_rms(x)).astype(BF16)
            for a, ref in enumerate((v_ref, g_ref)):
                out[pl.ds((4 * b + 2 + a) * length, length), :] = ref[:, cols]
        seg = seg_ref[...].astype(F32).astype(BF16)
        out[pl.ds(4 * count * length, SEG_ROWS), :] = jnp.broadcast_to(seg, (SEG_ROWS, length))


def pack(queries, keys, values, grad_out, segment, chunks):
    length = queries.shape[0]
    return pl.pallas_call(
        functools.partial(pack_kernel, chunks),
        out_shape=[
            jax.ShapeDtypeStruct((4 * count * length + SEG_ROWS, HD), BF16) for _, count in chunks
        ],
        name="pack",
    )(queries, keys, values, grad_out, segment.reshape(1, length))


def attend_kernel(n, length, count, *refs):
    refs = list(refs)
    len_ref = refs.pop(0)
    gathered = refs.pop(0)
    q_raw, k_raw, tk_ref, tv_ref = refs[:4]
    out_ref, gq_ref, gk_ref, gv_ref, gtk_ref, gtv_ref = refs[-18:-12]
    held, qx, kx, vx, gx, e_ref, dp_ref, dk_ref, dv_ref, dq_ref, att_ref, sems = refs[-12:]
    text_rows = tk_ref.shape[0]
    clips = len_ref.shape[0]
    per_clip = text_rows // clips
    video = n * length
    total = video + text_rows
    head = pl.program_id(0)
    rows_of = min(video, ROW_BLOCK)
    row_blocks = video // rows_of
    scale = 1.0 / math.sqrt(HD)
    exponent = scale * math.log2(math.e)
    seg_at = 4 * count * length

    @pl.when(head == 0)
    def _():
        me = lax.axis_index("ctx")
        def fetch(s, _):
            source = lax.rem(me + s, n)
            copy = pltpu.make_async_copy(gathered.at[source], held.at[s], sems.at[0])
            copy.start()
            copy.wait()
            return 0

        lax.fori_loop(0, n, fetch, 0)

        lane = lax.broadcasted_iota(jnp.int32, (length, HD), 1)
        sub = lax.broadcasted_iota(jnp.int32, (HD, length), 0).astype(F32)

        def mask_rows(s, _):
            seg = held[s, pl.ds(seg_at, SEG_ROWS), :].astype(F32)[0:1, :]
            onehot = jnp.where(jnp.broadcast_to(seg, (HD, length)) == sub, 1.0, 0.0).T
            rows = pl.ds(pl.multiple_of(s * length, length), length)
            qx[rows, HD:] = jnp.where(lane == clips, 1.0, onehot).astype(BF16)
            kx[rows, HD:] = jnp.where(lane < clips, (onehot - 1.0) * FAR, 0.0).astype(BF16)
            return 0

        lax.fori_loop(0, n, mask_rows, 0, unroll=n <= 4)
        lane = lax.broadcasted_iota(jnp.int32, (per_clip, HD), 1)
        place = lax.broadcasted_iota(jnp.int32, (per_clip, HD), 0)
        for c in range(clips):
            other = jnp.where((lane < clips) & (lane != c), -FAR, 0.0)
            dead = jnp.where((lane == clips) & (place >= len_ref[c]), -FAR, 0.0)
            kx[pl.ds(video + c * per_clip, per_clip), HD:] = (other + dead).astype(BF16)

    def place_rows(s, _):
        rows = pl.ds(pl.multiple_of(s * length, length), length)
        for a, (ref, cols) in enumerate(((qx, pl.ds(0, HD)), (kx, pl.ds(0, HD)), (vx, pl.ds(0, HD)), (gx, pl.ds(0, HD)))):
            at = pl.multiple_of((4 * head + a) * length, length)
            ref[rows, cols] = held[s, pl.ds(at, length), :]
        return 0

    lax.fori_loop(0, n, place_rows, 0, unroll=n <= 4)
    text = tk_ref[...].astype(F32)
    kx[pl.ds(video, text_rows), :HD] = (text * inverse_rms(text)).astype(BF16)
    vx[pl.ds(video, text_rows), :] = tv_ref[...]

    def rows_step(rb, first):
        rows = pl.ds(pl.multiple_of(rb * rows_of, rows_of), rows_of)
        q_all = qx[rows, :]
        q_here = qx[rows, :HD]
        g_here = gx[rows, :]

        def score(kb, sums):
            at = pl.ds(pl.multiple_of(kb * KEY_BLOCK, KEY_BLOCK), KEY_BLOCK)
            e = jnp.exp2(dot(kx[at, :], q_all, (1, 1)) * exponent)
            dp = dot(vx[at, :], g_here, (1, 1))
            e_ref[at, :] = e
            dp_ref[at, :] = dp
            shape = (KEY_BLOCK // 8, 8, rows_of)
            return (
                sums[0] + jnp.sum(e.reshape(shape), axis=0),
                sums[1] + jnp.sum((e * dp).reshape(shape), axis=0),
            )

        blocks = total // KEY_BLOCK
        zero = jnp.zeros((8, rows_of), F32)
        sums = lax.fori_loop(0, blocks, score, (zero, zero), unroll=blocks <= 8)
        inv = 1.0 / jnp.sum(sums[0], axis=0, keepdims=True)
        inner = jnp.sum(sums[1], axis=0, keepdims=True) * inv

        def add(ref, at, value):
            if row_blocks == 1:
                ref[at, :] = value
            else:
                ref[at, :] = jnp.where(rb == 0, value, ref[at, :] + value)

        def terms(at, cols):
            p = e_ref[at, cols] * inv[:, cols]
            ds = p * (dp_ref[at, cols] - inner[:, cols])
            return p.astype(BF16), ds.astype(BF16)

        everything = slice(0, rows_of)
        mine = slice(0, length)

        def query_side(at, p, ds, start):
            att = dot(p, vx[at, :], (0, 0))
            dq = dot(ds, kx[at, :HD], (0, 0))
            if start:
                att_ref[...] = att
                dq_ref[...] = dq
            else:
                att_ref[...] += att
                dq_ref[...] += dq

        def own_rows(at, p, ds, start=False):
            if row_blocks == 1:
                query_side(at, p[:, mine], ds[:, mine], start)
            else:

                @pl.when(rb == 0)
                def _():
                    query_side(at, p[:, mine], ds[:, mine], start)

        own = pl.ds(0, length)
        p, ds = terms(own, everything)
        add(dk_ref, own, dot(ds, q_here, (1, 0)))
        add(dv_ref, own, dot(p, g_here, (1, 0)))
        own_rows(own, p, ds, True)

        def others():
            def other(s, _):
                at = pl.ds(pl.multiple_of(s * length, length), length)
                p, ds = terms(at, mine)
                query_side(at, p, ds, False)
                return 0

            lax.fori_loop(1, n, other, 0, unroll=n <= 4)

        if row_blocks == 1:
            others()
        else:
            pl.when(rb == 0)(others)
        for c in range(text_rows // KEY_BLOCK):
            at = pl.ds(video + c * KEY_BLOCK, KEY_BLOCK)
            to = pl.ds(c * KEY_BLOCK, KEY_BLOCK)
            p, ds = terms(at, everything)
            add(gtk_ref, to, dot(ds, q_here, (1, 0)))
            add(gtv_ref, to, dot(p, g_here, (1, 0)))
            own_rows(at, p, ds)

    if row_blocks == 1:
        rows_step(0, True)
    else:

        def step(rb, _):
            rows_step(rb, False)
            return 0

        lax.fori_loop(0, row_blocks, step, 0)

    out_ref[...] = att_ref[...].astype(BF16)
    gq_ref[...] = norm_back(q_raw[...].astype(F32), dq_ref[...] * scale).astype(BF16)
    gk_ref[...] = norm_back(k_raw[...].astype(F32), dk_ref[...] * scale).astype(BF16)
    gv_ref[...] = dv_ref[...].astype(BF16)
    gtk_ref[...] = norm_back(tk_ref[...].astype(F32), gtk_ref[...] * scale)


def attend(n, chunk, text_len, gathered, queries, keys, text_keys, text_values, before):
    first, count = chunk
    length, width = queries.shape
    text_rows = text_keys.shape[0]
    video = n * length
    total = video + text_rows
    rows_of = min(video, ROW_BLOCK)
    anywhere = pl.BlockSpec(memory_space=pl.ANY)

    def column(rows):
        return pl.BlockSpec((rows, HD), lambda h: (0, first + h))

    in_specs = (
        [pl.BlockSpec(memory_space=pltpu.SMEM)]
        + [anywhere]
        + [column(length)] * 2
        + [column(text_rows)] * 2
        + [anywhere] * len(before)
    )
    out_rows = [length] * 4 + [text_rows] * 2
    out_types = [BF16] * 4 + [F32] * 2
    operands = [text_len, gathered, queries, keys, text_keys, text_values, *before]
    base = len(operands) - len(before)
    pairs = count * total * rows_of * (video // rows_of)
    return pl.pallas_call(
        functools.partial(attend_kernel, n, length, count),
        grid=(count,),
        in_specs=in_specs,
        out_specs=[column(rows) for rows in out_rows],
        out_shape=[
            jax.ShapeDtypeStruct((rows, width), dtype) for rows, dtype in zip(out_rows, out_types)
        ],
        scratch_shapes=[
            pltpu.VMEM((n, 4 * count * length + SEG_ROWS, HD), BF16),
            pltpu.VMEM((video, 2 * HD), BF16),
            pltpu.VMEM((total, 2 * HD), BF16),
            pltpu.VMEM((total, HD), BF16),
            pltpu.VMEM((video, HD), BF16),
            pltpu.VMEM((total, rows_of), F32),
            pltpu.VMEM((total, rows_of), F32),
            pltpu.VMEM((length, HD), F32),
            pltpu.VMEM((length, HD), F32),
            pltpu.VMEM((length, HD), F32),
            pltpu.VMEM((length, HD), F32),
            pltpu.SemaphoreType.DMA((1,)),
        ],
        input_output_aliases={base + i: i for i in range(len(before))},
        compiler_params=pltpu.CompilerParams(vmem_limit_bytes=56 * 1024 * 1024),
        cost_estimate=pl.CostEstimate(
            flops=12 * pairs * HD, bytes_accessed=count * 3 * 1024 * 1024, transcendentals=pairs
        ),
        name="attend",
    )(*operands)


def text_kernel(len_ref, tk_ref, tv_ref, kt_ref, vt_ref):
    text_rows, width = tk_ref.shape
    clips = len_ref.shape[0]
    per_clip = text_rows // clips
    lane = lax.broadcasted_iota(jnp.int32, (per_clip, HD), 1)
    place = lax.broadcasted_iota(jnp.int32, (per_clip, HD), 0)
    for c in range(clips):
        other = jnp.where((lane < clips) & (lane != c), -FAR, 0.0)
        dead = jnp.where((lane == clips) & (place >= len_ref[c]), -FAR, 0.0)
        mask = (other + dead).astype(BF16)
        rows = pl.ds(c * per_clip, per_clip)
        for h in range(width // HD):
            to = pl.ds(h * text_rows + c * per_clip, per_clip)
            x = tk_ref[rows, pl.ds(h * HD, HD)].astype(F32)
            kt_ref[to, :HD] = (x * inverse_rms(x)).astype(BF16)
            kt_ref[to, HD:] = mask
    vt_ref[...] = tv_ref[...]


def prepare_text(text_len, text_keys, text_values):
    text_rows, width = text_keys.shape
    whole = pl.BlockSpec(memory_space=pltpu.VMEM)
    return pl.pallas_call(
        text_kernel,
        in_specs=[pl.BlockSpec(memory_space=pltpu.SMEM), whole, whole],
        out_specs=[whole, whole],
        out_shape=[
            jax.ShapeDtypeStruct((width // HD * text_rows, 2 * HD), BF16),
            jax.ShapeDtypeStruct((text_rows, width), BF16),
        ],
        compiler_params=pltpu.CompilerParams(vmem_limit_bytes=12 * 1024 * 1024),
        cost_estimate=pl.CostEstimate(
            flops=8 * text_rows * width, bytes_accessed=6 * text_rows * width, transcendentals=0
        ),
        name="prepare_text",
    )(text_len, text_keys, text_values)


def line_kernel(first, count, clips, *refs):
    own, near, skip, far, last, kt, vt, q_any, k_any, t_any = refs[:10]
    out, gq, gk, gv, gtk, gtv = refs[-26:-20]
    (pick, qx, kx, vx, gx, qs, gs, e_row, e_col, e_text, d_row, d_col, d_text) = refs[-20:-7]
    raw_q, raw_k, raw_t, staged, staged_text, in_sems, out_sems = refs[-7:]
    length = raw_q.shape[1]
    text_rows = vt.shape[0]
    per_clip = text_rows // clips
    half = 2 * length
    video = 4 * length
    scale = 1.0 / math.sqrt(HD)
    exponent = scale * math.log2(math.e)
    seg_at = 4 * count * length

    fetches = []
    for b in range(count):
        cols = pl.ds((first + b) * HD, HD)
        for a, (source, target) in enumerate(((q_any, raw_q), (k_any, raw_k), (t_any, raw_t))):
            copy = pltpu.make_async_copy(source.at[:, cols], target.at[b], in_sems.at[3 * b + a])
            copy.start()
            fetches.append(copy)

    me = lax.axis_index("ctx")
    end = (me == 0) | (me == 3)

    @pl.when(end)
    def _():
        pick[...] = last[...]

    @pl.when(jnp.logical_not(end))
    def _():
        pick[...] = far[...]

    pieces = (own, near, skip, pick)
    lane = lax.broadcasted_iota(jnp.int32, (length, HD), 1)
    sub = lax.broadcasted_iota(jnp.int32, (HD, length), 0).astype(F32)
    tops = []
    for s, piece in enumerate(pieces):
        seg = piece[pl.ds(seg_at, SEG_ROWS), :].astype(F32)[0:1, :]
        tops.append(jnp.max(seg))
        onehot = jnp.where(jnp.broadcast_to(seg, (HD, length)) == sub, 1.0, 0.0).T
        rows = pl.ds(s * length, length)
        qx[rows, HD:] = jnp.where(lane == clips, 1.0, onehot).astype(BF16)
        kx[rows, HD:] = jnp.where(lane < clips, (onehot - 1.0) * FAR, 0.0).astype(BF16)
    flipped = me >= 2
    middle = jnp.where(
        flipped, jnp.maximum(tops[2], tops[3]), jnp.maximum(tops[0], tops[1])
    ).astype(jnp.int32)

    pairs = []
    for k in range(clips + 1):
        second = k > middle
        clip = jnp.where(second, k - 1, k)
        here = second == flipped
        at = pl.multiple_of(jnp.where(here, 0, half), half)
        pairs.append((clip, here, pl.ds(at, half)))

    def split_sum(x):
        return jnp.sum(x.reshape(x.shape[0] // 8, 8, x.shape[1]), axis=0)

    mine = slice(0, length)
    stores = []

    def put(source, target, cols, rows=None):
        to = target.at[:, cols] if rows is None else target.at[rows, cols]
        copy = pltpu.make_async_copy(source, to, out_sems.at[len(stores)])
        copy.start()
        stores.append(copy)

    for b in range(count):
        cols = pl.ds((first + b) * HD, HD)
        for s, piece in enumerate(pieces):
            rows = pl.ds(s * length, length)
            for a, (ref, to) in enumerate(((qx, pl.ds(0, HD)), (kx, pl.ds(0, HD)), (vx, pl.ds(0, HD)), (gx, pl.ds(0, HD)))):
                ref[rows, to] = piece[pl.ds((4 * b + a) * length, length), :]

        norm = [jnp.zeros((8, half), F32)] * 2
        mean = [jnp.zeros((8, half), F32)] * 2
        for j in range(2):
            for i in range(2):
                keys, rows = pl.ds(j * half, half), pl.ds(i * half, half)
                e = jnp.exp2(dot(kx[keys, :], qx[rows, :], (1, 1)) * exponent)
                dp = dot(vx[keys, :], gx[rows, :], (1, 1))
                norm[i] = norm[i] + split_sum(e)
                mean[i] = mean[i] + split_sum(e * dp)
                if j == 0:
                    e_row[:, rows] = e[mine, :].astype(BF16)
                    d_row[:, rows] = dp[mine, :]
                if i == 0:
                    e_col[keys, :] = e[:, mine].astype(BF16)
                    d_col[keys, :] = dp[:, mine]
        for k, (clip, here, rows) in enumerate(pairs):
            keys = pl.ds(pl.multiple_of((first + b) * text_rows + clip * per_clip, per_clip), per_clip)
            vals = pl.ds(pl.multiple_of(clip * per_clip, per_clip), per_clip)
            e = jnp.exp2(dot(kt[keys, :], qx[rows, :], (1, 1)) * exponent)
            dp = dot(vt[vals, cols], gx[rows, :], (1, 1))
            e_text[k] = e.astype(BF16)
            d_text[k] = dp
            for sums, part in ((norm, split_sum(e)), (mean, split_sum(e * dp))):
                sums[0] = sums[0] + jnp.where(here, part, 0.0)
                sums[1] = sums[1] + jnp.where(here, 0.0, part)

        inv = [1.0 / jnp.sum(x, axis=0, keepdims=True) for x in norm]
        inner = [jnp.sum(x, axis=0, keepdims=True) * y for x, y in zip(mean, inv)]
        turned = []
        for s in range(4):
            part = inv[s // 2][:, (s % 2) * length : (s % 2 + 1) * length]
            turned.append(jnp.broadcast_to(part, (HD, length)).T)
            rows = pl.ds(s * length, length)
            qs[rows, :] = (qx[rows, :HD].astype(F32) * (turned[s] * scale)).astype(BF16)
            gs[rows, :] = (gx[rows, :].astype(F32) * turned[s]).astype(BF16)

        att = jnp.zeros((length, HD), F32)
        dq = jnp.zeros((length, HD), F32)
        fetches[3 * b + 2].wait()
        before = None
        for k, (clip, here, rows) in enumerate(pairs):
            keys = pl.ds(pl.multiple_of((first + b) * text_rows + clip * per_clip, per_clip), per_clip)
            vals = pl.ds(pl.multiple_of(clip * per_clip, per_clip), per_clip)
            eb = e_text[k]
            away = jnp.where(here, inner[0], inner[1])
            ds = (eb.astype(F32) * (d_text[k] - away)).astype(BF16)
            dk = dot(ds, qs[rows, :], (1, 0))
            dv = dot(eb, gs[rows, :], (1, 0))
            att = att + jnp.where(here, dot(eb[:, mine], vt[vals, cols], (0, 0)), 0.0)
            dq = dq + jnp.where(here, dot(ds[:, mine], kt[keys, :HD], (0, 0)), 0.0)
            if before is not None:
                c = k - 1
                low, high = c <= middle, c >= middle
                to = pl.ds(c * per_clip, per_clip)
                total = jnp.where(low, before[0], 0.0) + jnp.where(high, dk, 0.0)
                staged_text[b, 0, to, :] = norm_back(raw_t[b, to, :].astype(F32), total)
                staged_text[b, 1, to, :] = jnp.where(low, before[1], 0.0) + jnp.where(high, dv, 0.0)
                put(staged_text.at[b, 0, to], gtk, cols, to)
                put(staged_text.at[b, 1, to], gtv, cols, to)
            before = (dk, dv)

        eb = e_row[...]
        inner_all = jnp.concatenate(inner, axis=1)
        ds = (eb.astype(F32) * (d_row[...] - inner_all)).astype(BF16)
        dk = dot(ds, qs[...], (1, 0))
        dv = dot(eb, gs[...], (1, 0))
        eb = e_col[...]
        ds = (eb.astype(F32) * (d_col[...] - inner[0][:, mine])).astype(BF16)
        att = att + dot(eb, vx[...], (0, 0))
        dq = dq + dot(ds, kx[:, :HD], (0, 0))
        fetches[3 * b].wait()
        fetches[3 * b + 1].wait()
        staged[b, 0] = (att * turned[0]).astype(BF16)
        staged[b, 1] = norm_back(raw_q[b].astype(F32), dq * (turned[0] * scale)).astype(BF16)
        staged[b, 2] = norm_back(raw_k[b].astype(F32), dk).astype(BF16)
        staged[b, 3] = dv.astype(BF16)
        for a, target in enumerate((out, gq, gk, gv)):
            put(staged.at[b, a], target, cols)
    for copy in stores:
        copy.wait()


def attend_line(chunk, clips, pieces, text, queries, keys, text_keys, before):
    first, count = chunk
    length, width = queries.shape
    text_rows = text_keys.shape[0]
    per_clip = text_rows // clips
    half, video = 2 * length, 4 * length
    anywhere = pl.BlockSpec(memory_space=pl.ANY)
    remote = pl.BlockSpec(memory_space=pltpu.HBM)
    held = pl.BlockSpec(memory_space=pltpu.VMEM)
    out_rows = [length] * 4 + [text_rows] * 2
    out_types = [BF16] * 4 + [F32] * 2
    operands = [*pieces, *text, queries, keys, text_keys, *before]
    base = len(operands) - len(before)
    work = count * video * (video + text_rows)
    return pl.pallas_call(
        functools.partial(line_kernel, first, count, clips),
        in_specs=[held] * 7 + [remote] * 3 + [remote] * len(before),
        out_specs=[remote] * 6,
        out_shape=[
            jax.ShapeDtypeStruct((rows, width), dtype) for rows, dtype in zip(out_rows, out_types)
        ],
        scratch_shapes=[
            pltpu.VMEM((4 * count * length + SEG_ROWS, HD), BF16),
            pltpu.VMEM((video, 2 * HD), BF16),
            pltpu.VMEM((video, 2 * HD), BF16),
            pltpu.VMEM((video, HD), BF16),
            pltpu.VMEM((video, HD), BF16),
            pltpu.VMEM((video, HD), BF16),
            pltpu.VMEM((video, HD), BF16),
            pltpu.VMEM((length, video), BF16),
            pltpu.VMEM((video, length), BF16),
            pltpu.VMEM((clips + 1, per_clip, half), BF16),
            pltpu.VMEM((length, video), F32),
            pltpu.VMEM((video, length), F32),
            pltpu.VMEM((clips + 1, per_clip, half), F32),
            pltpu.VMEM((count, length, HD), BF16),
            pltpu.VMEM((count, length, HD), BF16),
            pltpu.VMEM((count, text_rows, HD), BF16),
            pltpu.VMEM((count, 4, length, HD), BF16),
            pltpu.VMEM((count, 2, text_rows, HD), F32),
            pltpu.SemaphoreType.DMA((3 * count,)),
            pltpu.SemaphoreType.DMA((count * (2 * clips + 4),)),
        ],
        input_output_aliases={base + i: i for i in range(len(before))},
        compiler_params=pltpu.CompilerParams(vmem_limit_bytes=16 * 1024 * 1024),
        cost_estimate=pl.CostEstimate(
            flops=12 * work * HD, bytes_accessed=count * 2 * 1024 * 1024, transcendentals=work
        ),
        name="attend_line",
    )(*operands)


def shards(n, queries, keys, values, text_keys, text_values, segment, text_len, grad_out):
    heads = queries.shape[1] // HD
    half = max(heads // 2, 1)
    chunks = [(first, half) for first in range(0, heads, half)]
    payloads = pack(queries, keys, values, grad_out, segment, chunks)

    def send(x, pairs):
        return lax.ppermute(x, "ctx", pairs)

    if n == 4:
        outer = [(0, 1), (1, 0), (2, 3), (3, 2)]
        across = [(0, 2), (2, 0), (1, 3), (3, 1)]
        middle = [(1, 2), (2, 1)]
        outward = [(1, 0), (2, 3)]
        pieces = []
        for x in payloads:
            skip = send(x, across)
            near = send(x, outer)
            far = send(x, middle)
            last = send(skip, outward)
            pieces.append((x, near, skip, far, last))
        text = prepare_text(text_len, text_keys, text_values)
        outs = ()
        for chunk, piece in zip(chunks, pieces):
            outs = attend_line(
                chunk, text_len.shape[0], piece, text, queries, keys, text_keys, outs
            )
        return tuple(outs)
    outs = ()
    for chunk, x in zip(chunks, payloads):
        gathered = lax.all_gather(x, "ctx", axis=0)
        outs = attend(
            n, chunk, text_len, gathered, queries, keys, text_keys, text_values, outs
        )
    return tuple(outs)


def solution(mesh):
    rows = P(("groups", "ctx"), ("mp", "sec"))
    text = P("groups", ("mp", "sec"))
    in_specs = (rows, rows, rows, text, text, P(("groups", "ctx")), P("groups"), rows)
    out_specs = (rows, rows, rows, rows, text, text)
    return jax.shard_map(
        functools.partial(shards, mesh.shape["ctx"]),
        mesh=mesh,
        in_specs=in_specs,
        out_specs=out_specs,
        check_vma=False,
    )
```

```python
import functools
import math

import jax
import jax.numpy as jnp
from jax import lax
from jax.experimental import pallas as pl
from jax.experimental.pallas import tpu as pltpu
from jax.sharding import PartitionSpec as P

HD = 128
SEG_ROWS = 16
FAR = 16384.0
KEY_BLOCK = 256
ROW_BLOCK = 512

epsilon = 1e-06

F32 = jnp.float32
BF16 = jnp.bfloat16


def inverse_rms(x):
    return lax.rsqrt(jnp.mean(x * x, axis=-1, keepdims=True) + epsilon)


def norm_back(x, upstream):
    inverse = inverse_rms(x)
    inner = jnp.sum(upstream * x, axis=-1, keepdims=True) * (1.0 / HD)
    return upstream * inverse - x * (inner * inverse * inverse * inverse)


def dot(a, b, contract):
    return lax.dot_general(a, b, ((contract[:1], contract[1:]), ((), ())), preferred_element_type=F32)


def pack_kernel(chunks, q_ref, k_ref, v_ref, g_ref, seg_ref, *outs):
    length = q_ref.shape[0]
    for (first, count), out in zip(chunks, outs):
        for b in range(count):
            cols = pl.ds((first + b) * HD, HD)
            for a, ref in enumerate((q_ref, k_ref)):
                x = ref[:, cols].astype(F32)
                out[pl.ds((4 * b + a) * length, length), :] = (x * inverse_rms(x)).astype(BF16)
            for a, ref in enumerate((v_ref, g_ref)):
                out[pl.ds((4 * b + 2 + a) * length, length), :] = ref[:, cols]
        seg = seg_ref[...].astype(F32).astype(BF16)
        out[pl.ds(4 * count * length, SEG_ROWS), :] = jnp.broadcast_to(seg, (SEG_ROWS, length))


def pack(queries, keys, values, grad_out, segment, chunks):
    length = queries.shape[0]
    return pl.pallas_call(
        functools.partial(pack_kernel, chunks),
        out_shape=[
            jax.ShapeDtypeStruct((4 * count * length + SEG_ROWS, HD), BF16) for _, count in chunks
        ],
        name="pack",
    )(queries, keys, values, grad_out, segment.reshape(1, length))


def attend_kernel(n, length, count, *refs):
    refs = list(refs)
    len_ref = refs.pop(0)
    gathered = refs.pop(0)
    q_raw, k_raw, tk_ref, tv_ref = refs[:4]
    out_ref, gq_ref, gk_ref, gv_ref, gtk_ref, gtv_ref = refs[-18:-12]
    held, qx, kx, vx, gx, e_ref, dp_ref, dk_ref, dv_ref, dq_ref, att_ref, sems = refs[-12:]
    text_rows = tk_ref.shape[0]
    clips = len_ref.shape[0]
    per_clip = text_rows // clips
    video = n * length
    total = video + text_rows
    head = pl.program_id(0)
    rows_of = min(video, ROW_BLOCK)
    row_blocks = video // rows_of
    scale = 1.0 / math.sqrt(HD)
    exponent = scale * math.log2(math.e)
    seg_at = 4 * count * length

    @pl.when(head == 0)
    def _():
        me = lax.axis_index("ctx")
        def fetch(s, _):
            source = lax.rem(me + s, n)
            copy = pltpu.make_async_copy(gathered.at[source], held.at[s], sems.at[0])
            copy.start()
            copy.wait()
            return 0

        lax.fori_loop(0, n, fetch, 0)

        lane = lax.broadcasted_iota(jnp.int32, (length, HD), 1)
        sub = lax.broadcasted_iota(jnp.int32, (HD, length), 0).astype(F32)

        def mask_rows(s, _):
            seg = held[s, pl.ds(seg_at, SEG_ROWS), :].astype(F32)[0:1, :]
            onehot = jnp.where(jnp.broadcast_to(seg, (HD, length)) == sub, 1.0, 0.0).T
            rows = pl.ds(pl.multiple_of(s * length, length), length)
            qx[rows, HD:] = jnp.where(lane == clips, 1.0, onehot).astype(BF16)
            kx[rows, HD:] = jnp.where(lane < clips, (onehot - 1.0) * FAR, 0.0).astype(BF16)
            return 0

        lax.fori_loop(0, n, mask_rows, 0, unroll=n <= 4)
        lane = lax.broadcasted_iota(jnp.int32, (per_clip, HD), 1)
        place = lax.broadcasted_iota(jnp.int32, (per_clip, HD), 0)
        for c in range(clips):
            other = jnp.where((lane < clips) & (lane != c), -FAR, 0.0)
            dead = jnp.where((lane == clips) & (place >= len_ref[c]), -FAR, 0.0)
            kx[pl.ds(video + c * per_clip, per_clip), HD:] = (other + dead).astype(BF16)

    def place_rows(s, _):
        rows = pl.ds(pl.multiple_of(s * length, length), length)
        for a, (ref, cols) in enumerate(((qx, pl.ds(0, HD)), (kx, pl.ds(0, HD)), (vx, pl.ds(0, HD)), (gx, pl.ds(0, HD)))):
            at = pl.multiple_of((4 * head + a) * length, length)
            ref[rows, cols] = held[s, pl.ds(at, length), :]
        return 0

    lax.fori_loop(0, n, place_rows, 0, unroll=n <= 4)
    text = tk_ref[...].astype(F32)
    kx[pl.ds(video, text_rows), :HD] = (text * inverse_rms(text)).astype(BF16)
    vx[pl.ds(video, text_rows), :] = tv_ref[...]

    def rows_step(rb, first):
        rows = pl.ds(pl.multiple_of(rb * rows_of, rows_of), rows_of)
        q_all = qx[rows, :]
        q_here = qx[rows, :HD]
        g_here = gx[rows, :]

        def score(kb, sums):
            at = pl.ds(pl.multiple_of(kb * KEY_BLOCK, KEY_BLOCK), KEY_BLOCK)
            e = jnp.exp2(dot(kx[at, :], q_all, (1, 1)) * exponent)
            dp = dot(vx[at, :], g_here, (1, 1))
            e_ref[at, :] = e
            dp_ref[at, :] = dp
            shape = (KEY_BLOCK // 8, 8, rows_of)
            return (
                sums[0] + jnp.sum(e.reshape(shape), axis=0),
                sums[1] + jnp.sum((e * dp).reshape(shape), axis=0),
            )

        blocks = total // KEY_BLOCK
        zero = jnp.zeros((8, rows_of), F32)
        sums = lax.fori_loop(0, blocks, score, (zero, zero), unroll=blocks <= 8)
        inv = 1.0 / jnp.sum(sums[0], axis=0, keepdims=True)
        inner = jnp.sum(sums[1], axis=0, keepdims=True) * inv

        def add(ref, at, value):
            if row_blocks == 1:
                ref[at, :] = value
            else:
                ref[at, :] = jnp.where(rb == 0, value, ref[at, :] + value)

        def terms(at, cols):
            p = e_ref[at, cols] * inv[:, cols]
            ds = p * (dp_ref[at, cols] - inner[:, cols])
            return p.astype(BF16), ds.astype(BF16)

        everything = slice(0, rows_of)
        mine = slice(0, length)

        def query_side(at, p, ds, start):
            att = dot(p, vx[at, :], (0, 0))
            dq = dot(ds, kx[at, :HD], (0, 0))
            if start:
                att_ref[...] = att
                dq_ref[...] = dq
            else:
                att_ref[...] += att
                dq_ref[...] += dq

        def own_rows(at, p, ds, start=False):
            if row_blocks == 1:
                query_side(at, p[:, mine], ds[:, mine], start)
            else:

                @pl.when(rb == 0)
                def _():
                    query_side(at, p[:, mine], ds[:, mine], start)

        own = pl.ds(0, length)
        p, ds = terms(own, everything)
        add(dk_ref, own, dot(ds, q_here, (1, 0)))
        add(dv_ref, own, dot(p, g_here, (1, 0)))
        own_rows(own, p, ds, True)

        def others():
            def other(s, _):
                at = pl.ds(pl.multiple_of(s * length, length), length)
                p, ds = terms(at, mine)
                query_side(at, p, ds, False)
                return 0

            lax.fori_loop(1, n, other, 0, unroll=n <= 4)

        if row_blocks == 1:
            others()
        else:
            pl.when(rb == 0)(others)
        for c in range(text_rows // KEY_BLOCK):
            at = pl.ds(video + c * KEY_BLOCK, KEY_BLOCK)
            to = pl.ds(c * KEY_BLOCK, KEY_BLOCK)
            p, ds = terms(at, everything)
            add(gtk_ref, to, dot(ds, q_here, (1, 0)))
            add(gtv_ref, to, dot(p, g_here, (1, 0)))
            own_rows(at, p, ds)

    if row_blocks == 1:
        rows_step(0, True)
    else:

        def step(rb, _):
            rows_step(rb, False)
            return 0

        lax.fori_loop(0, row_blocks, step, 0)

    out_ref[...] = att_ref[...].astype(BF16)
    gq_ref[...] = norm_back(q_raw[...].astype(F32), dq_ref[...] * scale).astype(BF16)
    gk_ref[...] = norm_back(k_raw[...].astype(F32), dk_ref[...] * scale).astype(BF16)
    gv_ref[...] = dv_ref[...].astype(BF16)
    gtk_ref[...] = norm_back(tk_ref[...].astype(F32), gtk_ref[...] * scale)


def attend(n, chunk, text_len, gathered, queries, keys, text_keys, text_values, before):
    first, count = chunk
    length, width = queries.shape
    text_rows = text_keys.shape[0]
    video = n * length
    total = video + text_rows
    rows_of = min(video, ROW_BLOCK)
    anywhere = pl.BlockSpec(memory_space=pl.ANY)

    def column(rows):
        return pl.BlockSpec((rows, HD), lambda h: (0, first + h))

    in_specs = (
        [pl.BlockSpec(memory_space=pltpu.SMEM)]
        + [anywhere]
        + [column(length)] * 2
        + [column(text_rows)] * 2
        + [anywhere] * len(before)
    )
    out_rows = [length] * 4 + [text_rows] * 2
    out_types = [BF16] * 4 + [F32] * 2
    operands = [text_len, gathered, queries, keys, text_keys, text_values, *before]
    base = len(operands) - len(before)
    pairs = count * total * rows_of * (video // rows_of)
    return pl.pallas_call(
        functools.partial(attend_kernel, n, length, count),
        grid=(count,),
        in_specs=in_specs,
        out_specs=[column(rows) for rows in out_rows],
        out_shape=[
            jax.ShapeDtypeStruct((rows, width), dtype) for rows, dtype in zip(out_rows, out_types)
        ],
        scratch_shapes=[
            pltpu.VMEM((n, 4 * count * length + SEG_ROWS, HD), BF16),
            pltpu.VMEM((video, 2 * HD), BF16),
            pltpu.VMEM((total, 2 * HD), BF16),
            pltpu.VMEM((total, HD), BF16),
            pltpu.VMEM((video, HD), BF16),
            pltpu.VMEM((total, rows_of), F32),
            pltpu.VMEM((total, rows_of), F32),
            pltpu.VMEM((length, HD), F32),
            pltpu.VMEM((length, HD), F32),
            pltpu.VMEM((length, HD), F32),
            pltpu.VMEM((length, HD), F32),
            pltpu.SemaphoreType.DMA((1,)),
        ],
        input_output_aliases={base + i: i for i in range(len(before))},
        compiler_params=pltpu.CompilerParams(vmem_limit_bytes=56 * 1024 * 1024),
        cost_estimate=pl.CostEstimate(
            flops=12 * pairs * HD, bytes_accessed=count * 3 * 1024 * 1024, transcendentals=pairs
        ),
        name="attend",
    )(*operands)


def text_kernel(len_ref, tk_ref, tv_ref, kt_ref, vt_ref):
    text_rows, width = tk_ref.shape
    clips = len_ref.shape[0]
    per_clip = text_rows // clips
    lane = lax.broadcasted_iota(jnp.int32, (per_clip, HD), 1)
    place = lax.broadcasted_iota(jnp.int32, (per_clip, HD), 0)
    for c in range(clips):
        other = jnp.where((lane < clips) & (lane != c), -FAR, 0.0)
        dead = jnp.where((lane == clips) & (place >= len_ref[c]), -FAR, 0.0)
        mask = (other + dead).astype(BF16)
        rows = pl.ds(c * per_clip, per_clip)
        for h in range(width // HD):
            to = pl.ds(h * text_rows + c * per_clip, per_clip)
            x = tk_ref[rows, pl.ds(h * HD, HD)].astype(F32)
            kt_ref[to, :HD] = (x * inverse_rms(x)).astype(BF16)
            kt_ref[to, HD:] = mask
    vt_ref[...] = tv_ref[...]


def prepare_text(text_len, text_keys, text_values):
    text_rows, width = text_keys.shape
    whole = pl.BlockSpec(memory_space=pltpu.VMEM)
    return pl.pallas_call(
        text_kernel,
        in_specs=[pl.BlockSpec(memory_space=pltpu.SMEM), whole, whole],
        out_specs=[whole, whole],
        out_shape=[
            jax.ShapeDtypeStruct((width // HD * text_rows, 2 * HD), BF16),
            jax.ShapeDtypeStruct((text_rows, width), BF16),
        ],
        compiler_params=pltpu.CompilerParams(vmem_limit_bytes=12 * 1024 * 1024),
        cost_estimate=pl.CostEstimate(
            flops=8 * text_rows * width, bytes_accessed=6 * text_rows * width, transcendentals=0
        ),
        name="prepare_text",
    )(text_len, text_keys, text_values)


def line_kernel(first, count, clips, *refs):
    own, near, skip, far, last, kt, vt, q_any, k_any, t_any = refs[:10]
    out, gq, gk, gv, gtk, gtv = refs[-26:-20]
    (pick, qx, kx, vx, gx, qs, gs, e_row, e_col, e_text, d_row, d_col, d_text) = refs[-20:-7]
    raw_q, raw_k, raw_t, staged, staged_text, in_sems, out_sems = refs[-7:]
    length = raw_q.shape[1]
    text_rows = vt.shape[0]
    per_clip = text_rows // clips
    half = 2 * length
    video = 4 * length
    scale = 1.0 / math.sqrt(HD)
    exponent = scale * math.log2(math.e)
    seg_at = 4 * count * length

    fetches = []
    for b in range(count):
        cols = pl.ds((first + b) * HD, HD)
        for a, (source, target) in enumerate(((q_any, raw_q), (k_any, raw_k), (t_any, raw_t))):
            copy = pltpu.make_async_copy(source.at[:, cols], target.at[b], in_sems.at[3 * b + a])
            copy.start()
            fetches.append(copy)

    me = lax.axis_index("ctx")
    end = (me == 0) | (me == 3)

    @pl.when(end)
    def _():
        pick[...] = last[...]

    @pl.when(jnp.logical_not(end))
    def _():
        pick[...] = far[...]

    pieces = (own, near, skip, pick)
    lane = lax.broadcasted_iota(jnp.int32, (length, HD), 1)
    sub = lax.broadcasted_iota(jnp.int32, (HD, length), 0).astype(F32)
    tops = []
    for s, piece in enumerate(pieces):
        seg = piece[pl.ds(seg_at, SEG_ROWS), :].astype(F32)[0:1, :]
        tops.append(jnp.max(seg))
        onehot = jnp.where(jnp.broadcast_to(seg, (HD, length)) == sub, 1.0, 0.0).T
        rows = pl.ds(s * length, length)
        qx[rows, HD:] = jnp.where(lane == clips, 1.0, onehot).astype(BF16)
        kx[rows, HD:] = jnp.where(lane < clips, (onehot - 1.0) * FAR, 0.0).astype(BF16)
    flipped = me >= 2
    middle = jnp.where(
        flipped, jnp.maximum(tops[2], tops[3]), jnp.maximum(tops[0], tops[1])
    ).astype(jnp.int32)

    pairs = []
    for k in range(clips + 1):
        second = k > middle
        clip = jnp.where(second, k - 1, k)
        here = second == flipped
        at = pl.multiple_of(jnp.where(here, 0, half), half)
        pairs.append((clip, here, pl.ds(at, half)))

    def split_sum(x):
        return jnp.sum(x.reshape(x.shape[0] // 8, 8, x.shape[1]), axis=0)

    mine = slice(0, length)
    stores = []

    def put(source, target, cols, rows=None):
        to = target.at[:, cols] if rows is None else target.at[rows, cols]
        copy = pltpu.make_async_copy(source, to, out_sems.at[len(stores)])
        copy.start()
        stores.append(copy)

    for b in range(count):
        cols = pl.ds((first + b) * HD, HD)
        for s, piece in enumerate(pieces):
            rows = pl.ds(s * length, length)
            for a, (ref, to) in enumerate(((qx, pl.ds(0, HD)), (kx, pl.ds(0, HD)), (vx, pl.ds(0, HD)), (gx, pl.ds(0, HD)))):
                ref[rows, to] = piece[pl.ds((4 * b + a) * length, length), :]

        norm = [jnp.zeros((8, half), F32)] * 2
        mean = [jnp.zeros((8, half), F32)] * 2
        for j in range(2):
            for i in range(2):
                keys, rows = pl.ds(j * half, half), pl.ds(i * half, half)
                e = jnp.exp2(dot(kx[keys, :], qx[rows, :], (1, 1)) * exponent)
                dp = dot(vx[keys, :], gx[rows, :], (1, 1))
                norm[i] = norm[i] + split_sum(e)
                mean[i] = mean[i] + split_sum(e * dp)
                if j == 0:
                    e_row[:, rows] = e[mine, :].astype(BF16)
                    d_row[:, rows] = dp[mine, :]
                if i == 0:
                    e_col[keys, :] = e[:, mine].astype(BF16)
                    d_col[keys, :] = dp[:, mine]
        for k, (clip, here, rows) in enumerate(pairs):
            keys = pl.ds(pl.multiple_of((first + b) * text_rows + clip * per_clip, per_clip), per_clip)
            vals = pl.ds(pl.multiple_of(clip * per_clip, per_clip), per_clip)
            e = jnp.exp2(dot(kt[keys, :], qx[rows, :], (1, 1)) * exponent)
            dp = dot(vt[vals, cols], gx[rows, :], (1, 1))
            e_text[k] = e.astype(BF16)
            d_text[k] = dp
            for sums, part in ((norm, split_sum(e)), (mean, split_sum(e * dp))):
                sums[0] = sums[0] + jnp.where(here, part, 0.0)
                sums[1] = sums[1] + jnp.where(here, 0.0, part)

        inv = [1.0 / jnp.sum(x, axis=0, keepdims=True) for x in norm]
        inner = [jnp.sum(x, axis=0, keepdims=True) * y for x, y in zip(mean, inv)]
        turned = []
        for s in range(4):
            part = inv[s // 2][:, (s % 2) * length : (s % 2 + 1) * length]
            turned.append(jnp.broadcast_to(part, (HD, length)).T)
            rows = pl.ds(s * length, length)
            qs[rows, :] = (qx[rows, :HD].astype(F32) * (turned[s] * scale)).astype(BF16)
            gs[rows, :] = (gx[rows, :].astype(F32) * turned[s]).astype(BF16)

        att = jnp.zeros((length, HD), F32)
        dq = jnp.zeros((length, HD), F32)
        fetches[3 * b + 2].wait()
        before = None
        for k, (clip, here, rows) in enumerate(pairs):
            keys = pl.ds(pl.multiple_of((first + b) * text_rows + clip * per_clip, per_clip), per_clip)
            vals = pl.ds(pl.multiple_of(clip * per_clip, per_clip), per_clip)
            eb = e_text[k]
            away = jnp.where(here, inner[0], inner[1])
            ds = (eb.astype(F32) * (d_text[k] - away)).astype(BF16)
            dk = dot(ds, qs[rows, :], (1, 0))
            dv = dot(eb, gs[rows, :], (1, 0))
            att = att + jnp.where(here, dot(eb[:, mine], vt[vals, cols], (0, 0)), 0.0)
            dq = dq + jnp.where(here, dot(ds[:, mine], kt[keys, :HD], (0, 0)), 0.0)
            if before is not None:
                c = k - 1
                low, high = c <= middle, c >= middle
                to = pl.ds(c * per_clip, per_clip)
                total = jnp.where(low, before[0], 0.0) + jnp.where(high, dk, 0.0)
                staged_text[b, 0, to, :] = norm_back(raw_t[b, to, :].astype(F32), total)
                staged_text[b, 1, to, :] = jnp.where(low, before[1], 0.0) + jnp.where(high, dv, 0.0)
                put(staged_text.at[b, 0, to], gtk, cols, to)
                put(staged_text.at[b, 1, to], gtv, cols, to)
            before = (dk, dv)

        eb = e_row[...]
        inner_all = jnp.concatenate(inner, axis=1)
        ds = (eb.astype(F32) * (d_row[...] - inner_all)).astype(BF16)
        dk = dot(ds, qs[...], (1, 0))
        dv = dot(eb, gs[...], (1, 0))
        eb = e_col[...]
        ds = (eb.astype(F32) * (d_col[...] - inner[0][:, mine])).astype(BF16)
        att = att + dot(eb, vx[...], (0, 0))
        dq = dq + dot(ds, kx[:, :HD], (0, 0))
        fetches[3 * b].wait()
        fetches[3 * b + 1].wait()
        staged[b, 0] = (att * turned[0]).astype(BF16)
        staged[b, 1] = norm_back(raw_q[b].astype(F32), dq * (turned[0] * scale)).astype(BF16)
        staged[b, 2] = norm_back(raw_k[b].astype(F32), dk).astype(BF16)
        staged[b, 3] = dv.astype(BF16)
        for a, target in enumerate((out, gq, gk, gv)):
            put(staged.at[b, a], target, cols)
    for copy in stores:
        copy.wait()


def attend_line(chunk, clips, pieces, text, queries, keys, text_keys, before):
    first, count = chunk
    length, width = queries.shape
    text_rows = text_keys.shape[0]
    per_clip = text_rows // clips
    half, video = 2 * length, 4 * length
    anywhere = pl.BlockSpec(memory_space=pl.ANY)
    remote = pl.BlockSpec(memory_space=pltpu.HBM)
    held = pl.BlockSpec(memory_space=pltpu.VMEM)
    out_rows = [length] * 4 + [text_rows] * 2
    out_types = [BF16] * 4 + [F32] * 2
    operands = [*pieces, *text, queries, keys, text_keys, *before]
    base = len(operands) - len(before)
    work = count * video * (video + text_rows)
    return pl.pallas_call(
        functools.partial(line_kernel, first, count, clips),
        in_specs=[held] * 7 + [remote] * 3 + [remote] * len(before),
        out_specs=[remote] * 6,
        out_shape=[
            jax.ShapeDtypeStruct((rows, width), dtype) for rows, dtype in zip(out_rows, out_types)
        ],
        scratch_shapes=[
            pltpu.VMEM((4 * count * length + SEG_ROWS, HD), BF16),
            pltpu.VMEM((video, 2 * HD), BF16),
            pltpu.VMEM((video, 2 * HD), BF16),
            pltpu.VMEM((video, HD), BF16),
            pltpu.VMEM((video, HD), BF16),
            pltpu.VMEM((video, HD), BF16),
            pltpu.VMEM((video, HD), BF16),
            pltpu.VMEM((length, video), BF16),
            pltpu.VMEM((video, length), BF16),
            pltpu.VMEM((clips + 1, per_clip, half), BF16),
            pltpu.VMEM((length, video), F32),
            pltpu.VMEM((video, length), F32),
            pltpu.VMEM((clips + 1, per_clip, half), F32),
            pltpu.VMEM((count, length, HD), BF16),
            pltpu.VMEM((count, length, HD), BF16),
            pltpu.VMEM((count, text_rows, HD), BF16),
            pltpu.VMEM((count, 4, length, HD), BF16),
            pltpu.VMEM((count, 2, text_rows, HD), F32),
            pltpu.SemaphoreType.DMA((3 * count,)),
            pltpu.SemaphoreType.DMA((count * (2 * clips + 4),)),
        ],
        input_output_aliases={base + i: i for i in range(len(before))},
        compiler_params=pltpu.CompilerParams(vmem_limit_bytes=16 * 1024 * 1024),
        cost_estimate=pl.CostEstimate(
            flops=12 * work * HD, bytes_accessed=count * 2 * 1024 * 1024, transcendentals=work
        ),
        name="attend_line",
    )(*operands)


def shards(n, queries, keys, values, text_keys, text_values, segment, text_len, grad_out):
    heads = queries.shape[1] // HD
    half = max(heads // 2, 1)
    chunks = [(first, half) for first in range(0, heads, half)]
    payloads = pack(queries, keys, values, grad_out, segment, chunks)

    def send(x, pairs):
        return lax.ppermute(x, "ctx", pairs)

    if n == 4:
        outer = [(0, 1), (1, 0), (2, 3), (3, 2)]
        across = [(0, 2), (2, 0), (1, 3), (3, 1)]
        middle = [(1, 2), (2, 1)]
        outward = [(1, 0), (2, 3)]
        text = prepare_text(text_len, text_keys, text_values)

        def after(x, *others):
            return lax.optimization_barrier((x, *others))[0]

        a, b = payloads
        skip_a, near_a = send(a, across), send(a, outer)
        skip_b, near_b = send(b, across), send(b, outer)
        far_a, far_b = send(a, middle), send(b, middle)
        last_a = send(after(skip_a, near_b, *text), outward)
        last_b = send(skip_b, outward)
        pieces = [(a, near_a, skip_a, far_a, last_a), (b, near_b, skip_b, far_b, last_b)]
        outs = ()
        for chunk, piece in zip(chunks, pieces):
            outs = attend_line(
                chunk, text_len.shape[0], piece, text, queries, keys, text_keys, outs
            )
        return tuple(outs)
    outs = ()
    for chunk, x in zip(chunks, payloads):
        gathered = lax.all_gather(x, "ctx", axis=0)
        outs = attend(
            n, chunk, text_len, gathered, queries, keys, text_keys, text_values, outs
        )
    return tuple(outs)


def solution(mesh):
    rows = P(("groups", "ctx"), ("mp", "sec"))
    text = P("groups", ("mp", "sec"))
    in_specs = (rows, rows, rows, text, text, P(("groups", "ctx")), P("groups"), rows)
    out_specs = (rows, rows, rows, rows, text, text)
    return jax.shard_map(
        functools.partial(shards, mesh.shape["ctx"]),
        mesh=mesh,
        in_specs=in_specs,
        out_specs=out_specs,
        check_vma=False,
    )
```

```python
import functools
import math

import jax
import jax.numpy as jnp
from jax import lax
from jax.experimental import pallas as pl
from jax.experimental.pallas import tpu as pltpu
from jax.sharding import PartitionSpec as P

HD = 128
SEG_ROWS = 16
FAR = 16384.0
KEY_BLOCK = 256
ROW_BLOCK = 512

epsilon = 1e-06

F32 = jnp.float32
BF16 = jnp.bfloat16


def inverse_rms(x):
    return lax.rsqrt(jnp.mean(x * x, axis=-1, keepdims=True) + epsilon)


def norm_back(x, upstream):
    inverse = inverse_rms(x)
    inner = jnp.sum(upstream * x, axis=-1, keepdims=True) * (1.0 / HD)
    return upstream * inverse - x * (inner * inverse * inverse * inverse)


def dot(a, b, contract):
    return lax.dot_general(a, b, ((contract[:1], contract[1:]), ((), ())), preferred_element_type=F32)


def pack_kernel(chunks, q_ref, k_ref, v_ref, g_ref, seg_ref, *outs):
    length = q_ref.shape[0]
    for (first, count), out in zip(chunks, outs):
        for b in range(count):
            cols = pl.ds((first + b) * HD, HD)
            for a, ref in enumerate((q_ref, k_ref)):
                x = ref[:, cols].astype(F32)
                out[pl.ds((4 * b + a) * length, length), :] = (x * inverse_rms(x)).astype(BF16)
            for a, ref in enumerate((v_ref, g_ref)):
                out[pl.ds((4 * b + 2 + a) * length, length), :] = ref[:, cols]
        seg = seg_ref[...].astype(F32).astype(BF16)
        out[pl.ds(4 * count * length, SEG_ROWS), :] = jnp.broadcast_to(seg, (SEG_ROWS, length))


def pack(queries, keys, values, grad_out, segment, chunks):
    length = queries.shape[0]
    return pl.pallas_call(
        functools.partial(pack_kernel, chunks),
        out_shape=[
            jax.ShapeDtypeStruct((4 * count * length + SEG_ROWS, HD), BF16) for _, count in chunks
        ],
        name="pack",
    )(queries, keys, values, grad_out, segment.reshape(1, length))


def attend_kernel(n, length, count, *refs):
    refs = list(refs)
    len_ref = refs.pop(0)
    gathered = refs.pop(0)
    q_raw, k_raw, tk_ref, tv_ref = refs[:4]
    out_ref, gq_ref, gk_ref, gv_ref, gtk_ref, gtv_ref = refs[-18:-12]
    held, qx, kx, vx, gx, e_ref, dp_ref, dk_ref, dv_ref, dq_ref, att_ref, sems = refs[-12:]
    text_rows = tk_ref.shape[0]
    clips = len_ref.shape[0]
    per_clip = text_rows // clips
    video = n * length
    total = video + text_rows
    head = pl.program_id(0)
    rows_of = min(video, ROW_BLOCK)
    row_blocks = video // rows_of
    scale = 1.0 / math.sqrt(HD)
    exponent = scale * math.log2(math.e)
    seg_at = 4 * count * length

    @pl.when(head == 0)
    def _():
        me = lax.axis_index("ctx")
        def fetch(s, _):
            source = lax.rem(me + s, n)
            copy = pltpu.make_async_copy(gathered.at[source], held.at[s], sems.at[0])
            copy.start()
            copy.wait()
            return 0

        lax.fori_loop(0, n, fetch, 0)

        lane = lax.broadcasted_iota(jnp.int32, (length, HD), 1)
        sub = lax.broadcasted_iota(jnp.int32, (HD, length), 0).astype(F32)

        def mask_rows(s, _):
            seg = held[s, pl.ds(seg_at, SEG_ROWS), :].astype(F32)[0:1, :]
            onehot = jnp.where(jnp.broadcast_to(seg, (HD, length)) == sub, 1.0, 0.0).T
            rows = pl.ds(pl.multiple_of(s * length, length), length)
            qx[rows, HD:] = jnp.where(lane == clips, 1.0, onehot).astype(BF16)
            kx[rows, HD:] = jnp.where(lane < clips, (onehot - 1.0) * FAR, 0.0).astype(BF16)
            return 0

        lax.fori_loop(0, n, mask_rows, 0, unroll=n <= 4)
        lane = lax.broadcasted_iota(jnp.int32, (per_clip, HD), 1)
        place = lax.broadcasted_iota(jnp.int32, (per_clip, HD), 0)
        for c in range(clips):
            other = jnp.where((lane < clips) & (lane != c), -FAR, 0.0)
            dead = jnp.where((lane == clips) & (place >= len_ref[c]), -FAR, 0.0)
            kx[pl.ds(video + c * per_clip, per_clip), HD:] = (other + dead).astype(BF16)

    def place_rows(s, _):
        rows = pl.ds(pl.multiple_of(s * length, length), length)
        for a, (ref, cols) in enumerate(((qx, pl.ds(0, HD)), (kx, pl.ds(0, HD)), (vx, pl.ds(0, HD)), (gx, pl.ds(0, HD)))):
            at = pl.multiple_of((4 * head + a) * length, length)
            ref[rows, cols] = held[s, pl.ds(at, length), :]
        return 0

    lax.fori_loop(0, n, place_rows, 0, unroll=n <= 4)
    text = tk_ref[...].astype(F32)
    kx[pl.ds(video, text_rows), :HD] = (text * inverse_rms(text)).astype(BF16)
    vx[pl.ds(video, text_rows), :] = tv_ref[...]

    def rows_step(rb, first):
        rows = pl.ds(pl.multiple_of(rb * rows_of, rows_of), rows_of)
        q_all = qx[rows, :]
        q_here = qx[rows, :HD]
        g_here = gx[rows, :]

        def score(kb, sums):
            at = pl.ds(pl.multiple_of(kb * KEY_BLOCK, KEY_BLOCK), KEY_BLOCK)
            e = jnp.exp2(dot(kx[at, :], q_all, (1, 1)) * exponent)
            dp = dot(vx[at, :], g_here, (1, 1))
            e_ref[at, :] = e
            dp_ref[at, :] = dp
            shape = (KEY_BLOCK // 8, 8, rows_of)
            return (
                sums[0] + jnp.sum(e.reshape(shape), axis=0),
                sums[1] + jnp.sum((e * dp).reshape(shape), axis=0),
            )

        blocks = total // KEY_BLOCK
        zero = jnp.zeros((8, rows_of), F32)
        sums = lax.fori_loop(0, blocks, score, (zero, zero), unroll=blocks <= 8)
        inv = 1.0 / jnp.sum(sums[0], axis=0, keepdims=True)
        inner = jnp.sum(sums[1], axis=0, keepdims=True) * inv

        def add(ref, at, value):
            if row_blocks == 1:
                ref[at, :] = value
            else:
                ref[at, :] = jnp.where(rb == 0, value, ref[at, :] + value)

        def terms(at, cols):
            p = e_ref[at, cols] * inv[:, cols]
            ds = p * (dp_ref[at, cols] - inner[:, cols])
            return p.astype(BF16), ds.astype(BF16)

        everything = slice(0, rows_of)
        mine = slice(0, length)

        def query_side(at, p, ds, start):
            att = dot(p, vx[at, :], (0, 0))
            dq = dot(ds, kx[at, :HD], (0, 0))
            if start:
                att_ref[...] = att
                dq_ref[...] = dq
            else:
                att_ref[...] += att
                dq_ref[...] += dq

        def own_rows(at, p, ds, start=False):
            if row_blocks == 1:
                query_side(at, p[:, mine], ds[:, mine], start)
            else:

                @pl.when(rb == 0)
                def _():
                    query_side(at, p[:, mine], ds[:, mine], start)

        own = pl.ds(0, length)
        p, ds = terms(own, everything)
        add(dk_ref, own, dot(ds, q_here, (1, 0)))
        add(dv_ref, own, dot(p, g_here, (1, 0)))
        own_rows(own, p, ds, True)

        def others():
            def other(s, _):
                at = pl.ds(pl.multiple_of(s * length, length), length)
                p, ds = terms(at, mine)
                query_side(at, p, ds, False)
                return 0

            lax.fori_loop(1, n, other, 0, unroll=n <= 4)

        if row_blocks == 1:
            others()
        else:
            pl.when(rb == 0)(others)
        for c in range(text_rows // KEY_BLOCK):
            at = pl.ds(video + c * KEY_BLOCK, KEY_BLOCK)
            to = pl.ds(c * KEY_BLOCK, KEY_BLOCK)
            p, ds = terms(at, everything)
            add(gtk_ref, to, dot(ds, q_here, (1, 0)))
            add(gtv_ref, to, dot(p, g_here, (1, 0)))
            own_rows(at, p, ds)

    if row_blocks == 1:
        rows_step(0, True)
    else:

        def step(rb, _):
            rows_step(rb, False)
            return 0

        lax.fori_loop(0, row_blocks, step, 0)

    out_ref[...] = att_ref[...].astype(BF16)
    gq_ref[...] = norm_back(q_raw[...].astype(F32), dq_ref[...] * scale).astype(BF16)
    gk_ref[...] = norm_back(k_raw[...].astype(F32), dk_ref[...] * scale).astype(BF16)
    gv_ref[...] = dv_ref[...].astype(BF16)
    gtk_ref[...] = norm_back(tk_ref[...].astype(F32), gtk_ref[...] * scale)


def attend(n, chunk, text_len, gathered, queries, keys, text_keys, text_values, before):
    first, count = chunk
    length, width = queries.shape
    text_rows = text_keys.shape[0]
    video = n * length
    total = video + text_rows
    rows_of = min(video, ROW_BLOCK)
    anywhere = pl.BlockSpec(memory_space=pl.ANY)

    def column(rows):
        return pl.BlockSpec((rows, HD), lambda h: (0, first + h))

    in_specs = (
        [pl.BlockSpec(memory_space=pltpu.SMEM)]
        + [anywhere]
        + [column(length)] * 2
        + [column(text_rows)] * 2
        + [anywhere] * len(before)
    )
    out_rows = [length] * 4 + [text_rows] * 2
    out_types = [BF16] * 4 + [F32] * 2
    operands = [text_len, gathered, queries, keys, text_keys, text_values, *before]
    base = len(operands) - len(before)
    pairs = count * total * rows_of * (video // rows_of)
    return pl.pallas_call(
        functools.partial(attend_kernel, n, length, count),
        grid=(count,),
        in_specs=in_specs,
        out_specs=[column(rows) for rows in out_rows],
        out_shape=[
            jax.ShapeDtypeStruct((rows, width), dtype) for rows, dtype in zip(out_rows, out_types)
        ],
        scratch_shapes=[
            pltpu.VMEM((n, 4 * count * length + SEG_ROWS, HD), BF16),
            pltpu.VMEM((video, 2 * HD), BF16),
            pltpu.VMEM((total, 2 * HD), BF16),
            pltpu.VMEM((total, HD), BF16),
            pltpu.VMEM((video, HD), BF16),
            pltpu.VMEM((total, rows_of), F32),
            pltpu.VMEM((total, rows_of), F32),
            pltpu.VMEM((length, HD), F32),
            pltpu.VMEM((length, HD), F32),
            pltpu.VMEM((length, HD), F32),
            pltpu.VMEM((length, HD), F32),
            pltpu.SemaphoreType.DMA((1,)),
        ],
        input_output_aliases={base + i: i for i in range(len(before))},
        compiler_params=pltpu.CompilerParams(vmem_limit_bytes=56 * 1024 * 1024),
        cost_estimate=pl.CostEstimate(
            flops=12 * pairs * HD, bytes_accessed=count * 3 * 1024 * 1024, transcendentals=pairs
        ),
        name="attend",
    )(*operands)


def text_kernel(len_ref, tk_ref, tv_ref, kt_ref, vt_ref, inv_ref):
    text_rows, width = tk_ref.shape
    clips = len_ref.shape[0]
    per_clip = text_rows // clips
    lane = lax.broadcasted_iota(jnp.int32, (per_clip, HD), 1)
    place = lax.broadcasted_iota(jnp.int32, (per_clip, HD), 0)
    for c in range(clips):
        other = jnp.where((lane < clips) & (lane != c), -FAR, 0.0)
        dead = jnp.where((lane == clips) & (place >= len_ref[c]), -FAR, 0.0)
        mask = (other + dead).astype(BF16)
        rows = pl.ds(c * per_clip, per_clip)
        for h in range(width // HD):
            to = pl.ds(h * text_rows + c * per_clip, per_clip)
            x = tk_ref[rows, pl.ds(h * HD, HD)].astype(F32)
            inverse = inverse_rms(x)
            kt_ref[to, :HD] = (x * inverse).astype(BF16)
            kt_ref[to, HD:] = mask
            inv_ref[to, :] = jnp.broadcast_to(inverse, (per_clip, HD))
    vt_ref[...] = tv_ref[...]


def prepare_text(text_len, text_keys, text_values):
    text_rows, width = text_keys.shape
    whole = pl.BlockSpec(memory_space=pltpu.VMEM)
    return pl.pallas_call(
        text_kernel,
        in_specs=[pl.BlockSpec(memory_space=pltpu.SMEM), whole, whole],
        out_specs=[whole, whole, whole],
        out_shape=[
            jax.ShapeDtypeStruct((width // HD * text_rows, 2 * HD), BF16),
            jax.ShapeDtypeStruct((text_rows, width), BF16),
            jax.ShapeDtypeStruct((width // HD * text_rows, HD), F32),
        ],
        compiler_params=pltpu.CompilerParams(vmem_limit_bytes=16 * 1024 * 1024),
        cost_estimate=pl.CostEstimate(
            flops=8 * text_rows * width, bytes_accessed=6 * text_rows * width, transcendentals=0
        ),
        name="prepare_text",
    )(text_len, text_keys, text_values)


def line_kernel(first, count, clips, *refs):
    own, near, skip, far, last, kt, vt, inv_t, q_any, k_any, t_any = refs[:11]
    out, gq, gk, gv, gtk, gtv = refs[-26:-20]
    (pick, qx, kx, vx, gx, qs, gs, e_row, e_col, e_text, d_row, d_col, d_text) = refs[-20:-7]
    raw_q, raw_k, raw_t, staged, staged_text, in_sems, out_sems = refs[-7:]
    length = raw_q.shape[1]
    text_rows = vt.shape[0]
    per_clip = text_rows // clips
    half = 2 * length
    video = 4 * length
    scale = 1.0 / math.sqrt(HD)
    exponent = scale * math.log2(math.e)
    seg_at = 4 * count * length

    fetches = []
    for b in range(count):
        cols = pl.ds((first + b) * HD, HD)
        for a, (source, target) in enumerate(((q_any, raw_q), (k_any, raw_k), (t_any, raw_t))):
            copy = pltpu.make_async_copy(source.at[:, cols], target.at[b], in_sems.at[3 * b + a])
            copy.start()
            fetches.append(copy)

    me = lax.axis_index("ctx")
    end = (me == 0) | (me == 3)

    @pl.when(end)
    def _():
        pick[...] = last[...]

    @pl.when(jnp.logical_not(end))
    def _():
        pick[...] = far[...]

    pieces = (own, near, skip, pick)
    lane = lax.broadcasted_iota(jnp.int32, (length, HD), 1)
    sub = lax.broadcasted_iota(jnp.int32, (HD, length), 0).astype(F32)
    tops = []
    for s, piece in enumerate(pieces):
        seg = piece[pl.ds(seg_at, SEG_ROWS), :].astype(F32)[0:1, :]
        tops.append(jnp.max(seg))
        onehot = jnp.where(jnp.broadcast_to(seg, (HD, length)) == sub, 1.0, 0.0).T
        rows = pl.ds(s * length, length)
        q_mask = jnp.where(lane == clips, 1.0, onehot).astype(BF16)
        k_mask = jnp.where(lane < clips, (onehot - 1.0) * FAR, 0.0).astype(BF16)
        for b in range(count):
            qx[b, rows, HD:] = q_mask
            kx[b, rows, HD:] = k_mask
    flipped = me >= 2
    middle = jnp.where(
        flipped, jnp.maximum(tops[2], tops[3]), jnp.maximum(tops[0], tops[1])
    ).astype(jnp.int32)

    pairs = []
    for k in range(clips + 1):
        second = k > middle
        clip = jnp.where(second, k - 1, k)
        here = second == flipped
        at = pl.multiple_of(jnp.where(here, 0, half), half)
        pairs.append((clip, here, pl.ds(at, half)))

    def split_sum(x):
        return jnp.sum(x.reshape(x.shape[0] // 8, 8, x.shape[1]), axis=0)

    mine = slice(0, length)
    stores = []
    state = [{} for _ in range(count)]

    def columns(b):
        return pl.ds((first + b) * HD, HD)

    def put(source, target, b):
        copy = pltpu.make_async_copy(source, target.at[:, columns(b)], out_sems.at[len(stores)])
        copy.start()
        stores.append(copy)

    def text_at(b, clip):
        keys = pl.ds(pl.multiple_of((first + b) * text_rows + clip * per_clip, per_clip), per_clip)
        return keys, pl.ds(pl.multiple_of(clip * per_clip, per_clip), per_clip)

    def place(b):
        for s, piece in enumerate(pieces):
            rows = pl.ds(s * length, length)
            for a, ref in enumerate((qx, kx, vx, gx)):
                ref[b, rows, :HD] = piece[pl.ds((4 * b + a) * length, length), :]

    def video_scores(b):
        norm = [jnp.zeros((8, half), F32)] * 2
        mean = [jnp.zeros((8, half), F32)] * 2
        for j in range(2):
            for i in range(2):
                keys, rows = pl.ds(j * half, half), pl.ds(i * half, half)
                e = jnp.exp2(dot(kx[b, keys, :], qx[b, rows, :], (1, 1)) * exponent)
                dp = dot(vx[b, keys, :], gx[b, rows, :], (1, 1))
                norm[i] = norm[i] + split_sum(e)
                mean[i] = mean[i] + split_sum(e * dp)
                if j == 0:
                    e_row[b, :, rows] = e[mine, :].astype(BF16)
                    d_row[b, :, rows] = dp[mine, :]
                if i == 0:
                    e_col[b, keys, :] = e[:, mine].astype(BF16)
                    d_col[b, keys, :] = dp[:, mine]
        state[b].update(norm=norm, mean=mean)

    def text_scores(b, k):
        clip, here, rows = pairs[k]
        keys, vals = text_at(b, clip)
        e = jnp.exp2(dot(kt[keys, :], qx[b, rows, :], (1, 1)) * exponent)
        dp = dot(vt[vals, columns(b)], gx[b, rows, :], (1, 1))
        e_text[b, k] = e.astype(BF16)
        d_text[b, k] = dp
        for name, part in (("norm", split_sum(e)), ("mean", split_sum(e * dp))):
            sums = state[b][name]
            sums[0] = sums[0] + jnp.where(here, part, 0.0)
            sums[1] = sums[1] + jnp.where(here, 0.0, part)

    def close_sums(b):
        inv = [1.0 / jnp.sum(x, axis=0, keepdims=True) for x in state[b]["norm"]]
        inner = [jnp.sum(x, axis=0, keepdims=True) * y for x, y in zip(state[b]["mean"], inv)]
        for s in range(4):
            part = inv[s // 2][:, (s % 2) * length : (s % 2 + 1) * length]
            turned = jnp.broadcast_to(part, (HD, length)).T
            if s == 0:
                state[b]["turned"] = turned
            rows = pl.ds(s * length, length)
            qs[b, rows, :] = (qx[b, rows, :HD].astype(F32) * (turned * scale)).astype(BF16)
            gs[b, rows, :] = (gx[b, rows, :].astype(F32) * turned).astype(BF16)
        state[b].update(
            inner=inner, att=jnp.zeros((length, HD), F32), dq=jnp.zeros((length, HD), F32), before=None
        )

    def text_grads(b, k):
        me_b = state[b]
        clip, here, rows = pairs[k]
        keys, vals = text_at(b, clip)
        eb = e_text[b, k]
        away = jnp.where(here, me_b["inner"][0], me_b["inner"][1])
        ds = (eb.astype(F32) * (d_text[b, k] - away)).astype(BF16)
        dk = dot(ds, qs[b, rows, :], (1, 0))
        dv = dot(eb, gs[b, rows, :], (1, 0))
        me_b["att"] += jnp.where(here, dot(eb[:, mine], vt[vals, columns(b)], (0, 0)), 0.0)
        me_b["dq"] += jnp.where(here, dot(ds[:, mine], kt[keys, :HD], (0, 0)), 0.0)
        if k:
            c = k - 1
            low, high = c <= middle, c >= middle
            to = pl.ds(c * per_clip, per_clip)
            total = jnp.where(low, me_b["before"][0], 0.0) + jnp.where(high, dk, 0.0)
            x = raw_t[b, to, :].astype(F32)
            inverse = inv_t[pl.ds((first + b) * text_rows + c * per_clip, per_clip), :]
            along = jnp.sum(total * x, axis=-1, keepdims=True)
            staged_text[b, 0, to, :] = inverse * (
                total - x * (along * (inverse * inverse * (1.0 / HD)))
            )
            staged_text[b, 1, to, :] = jnp.where(low, me_b["before"][1], 0.0) + jnp.where(high, dv, 0.0)
        me_b["before"] = (dk, dv)

    def put_text(b):
        put(staged_text.at[b, 0], gtk, b)
        put(staged_text.at[b, 1], gtv, b)

    def video_grads(b):
        me_b = state[b]
        eb = e_row[b]
        inner_all = jnp.concatenate(me_b["inner"], axis=1)
        ds = (eb.astype(F32) * (d_row[b] - inner_all)).astype(BF16)
        dk = dot(ds, qs[b], (1, 0))
        dv = dot(eb, gs[b], (1, 0))
        eb = e_col[b]
        ds = (eb.astype(F32) * (d_col[b] - me_b["inner"][0][:, mine])).astype(BF16)
        att = me_b["att"] + dot(eb, vx[b], (0, 0))
        dq = me_b["dq"] + dot(ds, kx[b, :, :HD], (0, 0))
        turned = me_b["turned"]
        staged[b, 0] = (att * turned).astype(BF16)
        staged[b, 1] = norm_back(raw_q[b].astype(F32), dq * (turned * scale)).astype(BF16)
        staged[b, 2] = norm_back(raw_k[b].astype(F32), dk).astype(BF16)
        staged[b, 3] = dv.astype(BF16)

    def put_rows(b):
        for a, target in enumerate((out, gq, gk, gv)):
            put(staged.at[b, a], target, b)

    for b in range(count):
        place(b)
        video_scores(b)
        for k in range(clips + 1):
            text_scores(b, k)
        close_sums(b)
        for a in range(3):
            fetches[3 * b + a].wait()
        for k in range(clips + 1):
            text_grads(b, k)
        video_grads(b)
        put_text(b)
        put_rows(b)
    for copy in stores:
        copy.wait()


def attend_line(chunk, clips, pieces, text, queries, keys, text_keys, before):
    first, count = chunk
    length, width = queries.shape
    text_rows = text_keys.shape[0]
    per_clip = text_rows // clips
    half, video = 2 * length, 4 * length
    anywhere = pl.BlockSpec(memory_space=pl.ANY)
    remote = pl.BlockSpec(memory_space=pltpu.HBM)
    held = pl.BlockSpec(memory_space=pltpu.VMEM)
    out_rows = [length] * 4 + [text_rows] * 2
    out_types = [BF16] * 4 + [F32] * 2
    operands = [*pieces, *text, queries, keys, text_keys, *before]
    base = len(operands) - len(before)
    work = count * video * (video + text_rows)
    return pl.pallas_call(
        functools.partial(line_kernel, first, count, clips),
        in_specs=[held] * 8 + [remote] * 3 + [remote] * len(before),
        out_specs=[remote] * 6,
        out_shape=[
            jax.ShapeDtypeStruct((rows, width), dtype) for rows, dtype in zip(out_rows, out_types)
        ],
        scratch_shapes=[
            pltpu.VMEM((4 * count * length + SEG_ROWS, HD), BF16),
            pltpu.VMEM((count, video, 2 * HD), BF16),
            pltpu.VMEM((count, video, 2 * HD), BF16),
            pltpu.VMEM((count, video, HD), BF16),
            pltpu.VMEM((count, video, HD), BF16),
            pltpu.VMEM((count, video, HD), BF16),
            pltpu.VMEM((count, video, HD), BF16),
            pltpu.VMEM((count, length, video), BF16),
            pltpu.VMEM((count, video, length), BF16),
            pltpu.VMEM((count, clips + 1, per_clip, half), BF16),
            pltpu.VMEM((count, length, video), F32),
            pltpu.VMEM((count, video, length), F32),
            pltpu.VMEM((count, clips + 1, per_clip, half), F32),
            pltpu.VMEM((count, length, HD), BF16),
            pltpu.VMEM((count, length, HD), BF16),
            pltpu.VMEM((count, text_rows, HD), BF16),
            pltpu.VMEM((count, 4, length, HD), BF16),
            pltpu.VMEM((count, 2, text_rows, HD), F32),
            pltpu.SemaphoreType.DMA((3 * count,)),
            pltpu.SemaphoreType.DMA((6 * count,)),
        ],
        input_output_aliases={base + i: i for i in range(len(before))},
        compiler_params=pltpu.CompilerParams(vmem_limit_bytes=16 * 1024 * 1024),
        cost_estimate=pl.CostEstimate(
            flops=12 * work * HD, bytes_accessed=count * 2 * 1024 * 1024, transcendentals=work
        ),
        name="attend_line",
    )(*operands)


def shards(n, queries, keys, values, text_keys, text_values, segment, text_len, grad_out):
    heads = queries.shape[1] // HD
    half = max(heads // 2, 1)
    chunks = [(first, half) for first in range(0, heads, half)]
    payloads = pack(queries, keys, values, grad_out, segment, chunks)

    def send(x, pairs):
        return lax.ppermute(x, "ctx", pairs)

    if n == 4:
        outer = [(0, 1), (1, 0), (2, 3), (3, 2)]
        across = [(0, 2), (2, 0), (1, 3), (3, 1)]
        middle = [(1, 2), (2, 1)]
        outward = [(1, 0), (2, 3)]
        text = prepare_text(text_len, text_keys, text_values)

        def after(x, *others):
            return lax.optimization_barrier((x, *others))[0]

        a, b = payloads
        skip_a, near_a = send(a, across), send(a, outer)
        skip_b, near_b = send(b, across), send(b, outer)
        far_a, far_b = send(a, middle), send(b, middle)
        last_a = send(after(skip_a, near_b, *text), outward)
        last_b = send(skip_b, outward)
        pieces = [(a, near_a, skip_a, far_a, last_a), (b, near_b, skip_b, far_b, last_b)]
        outs = ()
        for chunk, piece in zip(chunks, pieces):
            outs = attend_line(
                chunk, text_len.shape[0], piece, text, queries, keys, text_keys, outs
            )
        return tuple(outs)
    outs = ()
    for chunk, x in zip(chunks, payloads):
        gathered = lax.all_gather(x, "ctx", axis=0)
        outs = attend(
            n, chunk, text_len, gathered, queries, keys, text_keys, text_values, outs
        )
    return tuple(outs)


def solution(mesh):
    rows = P(("groups", "ctx"), ("mp", "sec"))
    text = P("groups", ("mp", "sec"))
    in_specs = (rows, rows, rows, text, text, P(("groups", "ctx")), P("groups"), rows)
    out_specs = (rows, rows, rows, rows, text, text)
    return jax.shard_map(
        functools.partial(shards, mesh.shape["ctx"]),
        mesh=mesh,
        in_specs=in_specs,
        out_specs=out_specs,
        check_vma=False,
    )
```

```python
import functools
import math

import jax
import jax.numpy as jnp
from jax import lax
from jax.experimental import pallas as pl
from jax.experimental.pallas import tpu as pltpu
from jax.sharding import PartitionSpec as P

HD = 128
SEG_ROWS = 16
FAR = 16384.0
KEY_BLOCK = 256
ROW_BLOCK = 512

epsilon = 1e-06

F32 = jnp.float32
BF16 = jnp.bfloat16


def inverse_rms(x):
    return lax.rsqrt(jnp.mean(x * x, axis=-1, keepdims=True) + epsilon)


def norm_back(x, upstream):
    inverse = inverse_rms(x)
    inner = jnp.sum(upstream * x, axis=-1, keepdims=True) * (1.0 / HD)
    return upstream * inverse - x * (inner * inverse * inverse * inverse)


def dot(a, b, contract):
    return lax.dot_general(a, b, ((contract[:1], contract[1:]), ((), ())), preferred_element_type=F32)


def pack_kernel(chunks, q_ref, k_ref, v_ref, g_ref, seg_ref, *outs):
    length = q_ref.shape[0]
    for (first, count), out in zip(chunks, outs):
        for b in range(count):
            cols = pl.ds((first + b) * HD, HD)
            for a, ref in enumerate((q_ref, k_ref)):
                x = ref[:, cols].astype(F32)
                out[pl.ds((4 * b + a) * length, length), :] = (x * inverse_rms(x)).astype(BF16)
            for a, ref in enumerate((v_ref, g_ref)):
                out[pl.ds((4 * b + 2 + a) * length, length), :] = ref[:, cols]
        seg = seg_ref[...].astype(F32).astype(BF16)
        out[pl.ds(4 * count * length, SEG_ROWS), :] = jnp.broadcast_to(seg, (SEG_ROWS, length))


def pack(queries, keys, values, grad_out, segment, chunks):
    length = queries.shape[0]
    return pl.pallas_call(
        functools.partial(pack_kernel, chunks),
        out_shape=[
            jax.ShapeDtypeStruct((4 * count * length + SEG_ROWS, HD), BF16) for _, count in chunks
        ],
        name="pack",
    )(queries, keys, values, grad_out, segment.reshape(1, length))


def attend_kernel(n, length, count, *refs):
    refs = list(refs)
    len_ref = refs.pop(0)
    gathered = refs.pop(0)
    q_raw, k_raw, tk_ref, tv_ref = refs[:4]
    out_ref, gq_ref, gk_ref, gv_ref, gtk_ref, gtv_ref = refs[-18:-12]
    held, qx, kx, vx, gx, e_ref, dp_ref, dk_ref, dv_ref, dq_ref, att_ref, sems = refs[-12:]
    text_rows = tk_ref.shape[0]
    clips = len_ref.shape[0]
    per_clip = text_rows // clips
    video = n * length
    total = video + text_rows
    head = pl.program_id(0)
    rows_of = min(video, ROW_BLOCK)
    row_blocks = video // rows_of
    scale = 1.0 / math.sqrt(HD)
    exponent = scale * math.log2(math.e)
    seg_at = 4 * count * length

    @pl.when(head == 0)
    def _():
        me = lax.axis_index("ctx")
        def fetch(s, _):
            source = lax.rem(me + s, n)
            copy = pltpu.make_async_copy(gathered.at[source], held.at[s], sems.at[0])
            copy.start()
            copy.wait()
            return 0

        lax.fori_loop(0, n, fetch, 0)

        lane = lax.broadcasted_iota(jnp.int32, (length, HD), 1)
        sub = lax.broadcasted_iota(jnp.int32, (HD, length), 0).astype(F32)

        def mask_rows(s, _):
            seg = held[s, pl.ds(seg_at, SEG_ROWS), :].astype(F32)[0:1, :]
            onehot = jnp.where(jnp.broadcast_to(seg, (HD, length)) == sub, 1.0, 0.0).T
            rows = pl.ds(pl.multiple_of(s * length, length), length)
            qx[rows, HD:] = jnp.where(lane == clips, 1.0, onehot).astype(BF16)
            kx[rows, HD:] = jnp.where(lane < clips, (onehot - 1.0) * FAR, 0.0).astype(BF16)
            return 0

        lax.fori_loop(0, n, mask_rows, 0, unroll=n <= 4)
        lane = lax.broadcasted_iota(jnp.int32, (per_clip, HD), 1)
        place = lax.broadcasted_iota(jnp.int32, (per_clip, HD), 0)
        for c in range(clips):
            other = jnp.where((lane < clips) & (lane != c), -FAR, 0.0)
            dead = jnp.where((lane == clips) & (place >= len_ref[c]), -FAR, 0.0)
            kx[pl.ds(video + c * per_clip, per_clip), HD:] = (other + dead).astype(BF16)

    def place_rows(s, _):
        rows = pl.ds(pl.multiple_of(s * length, length), length)
        for a, (ref, cols) in enumerate(((qx, pl.ds(0, HD)), (kx, pl.ds(0, HD)), (vx, pl.ds(0, HD)), (gx, pl.ds(0, HD)))):
            at = pl.multiple_of((4 * head + a) * length, length)
            ref[rows, cols] = held[s, pl.ds(at, length), :]
        return 0

    lax.fori_loop(0, n, place_rows, 0, unroll=n <= 4)
    text = tk_ref[...].astype(F32)
    kx[pl.ds(video, text_rows), :HD] = (text * inverse_rms(text)).astype(BF16)
    vx[pl.ds(video, text_rows), :] = tv_ref[...]

    def rows_step(rb, first):
        rows = pl.ds(pl.multiple_of(rb * rows_of, rows_of), rows_of)
        q_all = qx[rows, :]
        q_here = qx[rows, :HD]
        g_here = gx[rows, :]

        def score(kb, sums):
            at = pl.ds(pl.multiple_of(kb * KEY_BLOCK, KEY_BLOCK), KEY_BLOCK)
            e = jnp.exp2(dot(kx[at, :], q_all, (1, 1)) * exponent)
            dp = dot(vx[at, :], g_here, (1, 1))
            e_ref[at, :] = e
            dp_ref[at, :] = dp
            shape = (KEY_BLOCK // 8, 8, rows_of)
            return (
                sums[0] + jnp.sum(e.reshape(shape), axis=0),
                sums[1] + jnp.sum((e * dp).reshape(shape), axis=0),
            )

        blocks = total // KEY_BLOCK
        zero = jnp.zeros((8, rows_of), F32)
        sums = lax.fori_loop(0, blocks, score, (zero, zero), unroll=blocks <= 8)
        inv = 1.0 / jnp.sum(sums[0], axis=0, keepdims=True)
        inner = jnp.sum(sums[1], axis=0, keepdims=True) * inv

        def add(ref, at, value):
            if row_blocks == 1:
                ref[at, :] = value
            else:
                ref[at, :] = jnp.where(rb == 0, value, ref[at, :] + value)

        def terms(at, cols):
            p = e_ref[at, cols] * inv[:, cols]
            ds = p * (dp_ref[at, cols] - inner[:, cols])
            return p.astype(BF16), ds.astype(BF16)

        everything = slice(0, rows_of)
        mine = slice(0, length)

        def query_side(at, p, ds, start):
            att = dot(p, vx[at, :], (0, 0))
            dq = dot(ds, kx[at, :HD], (0, 0))
            if start:
                att_ref[...] = att
                dq_ref[...] = dq
            else:
                att_ref[...] += att
                dq_ref[...] += dq

        def own_rows(at, p, ds, start=False):
            if row_blocks == 1:
                query_side(at, p[:, mine], ds[:, mine], start)
            else:

                @pl.when(rb == 0)
                def _():
                    query_side(at, p[:, mine], ds[:, mine], start)

        own = pl.ds(0, length)
        p, ds = terms(own, everything)
        add(dk_ref, own, dot(ds, q_here, (1, 0)))
        add(dv_ref, own, dot(p, g_here, (1, 0)))
        own_rows(own, p, ds, True)

        def others():
            def other(s, _):
                at = pl.ds(pl.multiple_of(s * length, length), length)
                p, ds = terms(at, mine)
                query_side(at, p, ds, False)
                return 0

            lax.fori_loop(1, n, other, 0, unroll=n <= 4)

        if row_blocks == 1:
            others()
        else:
            pl.when(rb == 0)(others)
        for c in range(text_rows // KEY_BLOCK):
            at = pl.ds(video + c * KEY_BLOCK, KEY_BLOCK)
            to = pl.ds(c * KEY_BLOCK, KEY_BLOCK)
            p, ds = terms(at, everything)
            add(gtk_ref, to, dot(ds, q_here, (1, 0)))
            add(gtv_ref, to, dot(p, g_here, (1, 0)))
            own_rows(at, p, ds)

    if row_blocks == 1:
        rows_step(0, True)
    else:

        def step(rb, _):
            rows_step(rb, False)
            return 0

        lax.fori_loop(0, row_blocks, step, 0)

    out_ref[...] = att_ref[...].astype(BF16)
    gq_ref[...] = norm_back(q_raw[...].astype(F32), dq_ref[...] * scale).astype(BF16)
    gk_ref[...] = norm_back(k_raw[...].astype(F32), dk_ref[...] * scale).astype(BF16)
    gv_ref[...] = dv_ref[...].astype(BF16)
    gtk_ref[...] = norm_back(tk_ref[...].astype(F32), gtk_ref[...] * scale)


def attend(n, chunk, text_len, gathered, queries, keys, text_keys, text_values, before):
    first, count = chunk
    length, width = queries.shape
    text_rows = text_keys.shape[0]
    video = n * length
    total = video + text_rows
    rows_of = min(video, ROW_BLOCK)
    anywhere = pl.BlockSpec(memory_space=pl.ANY)

    def column(rows):
        return pl.BlockSpec((rows, HD), lambda h: (0, first + h))

    in_specs = (
        [pl.BlockSpec(memory_space=pltpu.SMEM)]
        + [anywhere]
        + [column(length)] * 2
        + [column(text_rows)] * 2
        + [anywhere] * len(before)
    )
    out_rows = [length] * 4 + [text_rows] * 2
    out_types = [BF16] * 4 + [F32] * 2
    operands = [text_len, gathered, queries, keys, text_keys, text_values, *before]
    base = len(operands) - len(before)
    pairs = count * total * rows_of * (video // rows_of)
    return pl.pallas_call(
        functools.partial(attend_kernel, n, length, count),
        grid=(count,),
        in_specs=in_specs,
        out_specs=[column(rows) for rows in out_rows],
        out_shape=[
            jax.ShapeDtypeStruct((rows, width), dtype) for rows, dtype in zip(out_rows, out_types)
        ],
        scratch_shapes=[
            pltpu.VMEM((n, 4 * count * length + SEG_ROWS, HD), BF16),
            pltpu.VMEM((video, 2 * HD), BF16),
            pltpu.VMEM((total, 2 * HD), BF16),
            pltpu.VMEM((total, HD), BF16),
            pltpu.VMEM((video, HD), BF16),
            pltpu.VMEM((total, rows_of), F32),
            pltpu.VMEM((total, rows_of), F32),
            pltpu.VMEM((length, HD), F32),
            pltpu.VMEM((length, HD), F32),
            pltpu.VMEM((length, HD), F32),
            pltpu.VMEM((length, HD), F32),
            pltpu.SemaphoreType.DMA((1,)),
        ],
        input_output_aliases={base + i: i for i in range(len(before))},
        compiler_params=pltpu.CompilerParams(vmem_limit_bytes=56 * 1024 * 1024),
        cost_estimate=pl.CostEstimate(
            flops=12 * pairs * HD, bytes_accessed=count * 3 * 1024 * 1024, transcendentals=pairs
        ),
        name="attend",
    )(*operands)


def text_kernel(len_ref, tk_ref, tv_ref, kt_ref, vt_ref, inv_ref):
    text_rows, width = tk_ref.shape
    clips = len_ref.shape[0]
    per_clip = text_rows // clips
    lane = lax.broadcasted_iota(jnp.int32, (per_clip, HD), 1)
    place = lax.broadcasted_iota(jnp.int32, (per_clip, HD), 0)
    for c in range(clips):
        other = jnp.where((lane < clips) & (lane != c), -FAR, 0.0)
        dead = jnp.where((lane == clips) & (place >= len_ref[c]), -FAR, 0.0)
        mask = (other + dead).astype(BF16)
        rows = pl.ds(c * per_clip, per_clip)
        for h in range(width // HD):
            to = pl.ds(h * text_rows + c * per_clip, per_clip)
            x = tk_ref[rows, pl.ds(h * HD, HD)].astype(F32)
            inverse = inverse_rms(x)
            kt_ref[to, :HD] = (x * inverse).astype(BF16)
            kt_ref[to, HD:] = mask
            inv_ref[to, :] = jnp.broadcast_to(inverse, (per_clip, HD))
    vt_ref[...] = tv_ref[...]


def prepare_text(text_len, text_keys, text_values):
    text_rows, width = text_keys.shape
    whole = pl.BlockSpec(memory_space=pltpu.VMEM)
    return pl.pallas_call(
        text_kernel,
        in_specs=[pl.BlockSpec(memory_space=pltpu.SMEM), whole, whole],
        out_specs=[whole, whole, whole],
        out_shape=[
            jax.ShapeDtypeStruct((width // HD * text_rows, 2 * HD), BF16),
            jax.ShapeDtypeStruct((text_rows, width), BF16),
            jax.ShapeDtypeStruct((width // HD * text_rows, HD), F32),
        ],
        compiler_params=pltpu.CompilerParams(vmem_limit_bytes=16 * 1024 * 1024),
        cost_estimate=pl.CostEstimate(
            flops=8 * text_rows * width, bytes_accessed=6 * text_rows * width, transcendentals=0
        ),
        name="prepare_text",
    )(text_len, text_keys, text_values)


def line_kernel(first, count, clips, *refs):
    own, near, skip, far, last, kt, vt, inv_t, q_any, k_any, t_any = refs[:11]
    out, gq, gk, gv, gtk, gtv = refs[-26:-20]
    (pick, qx, kx, vx, gx, qs, gs, e_row, e_col, e_text, d_row, d_col, d_text) = refs[-20:-7]
    raw_q, raw_k, raw_t, staged, staged_text, in_sems, out_sems = refs[-7:]
    length = raw_q.shape[1]
    text_rows = vt.shape[0]
    per_clip = text_rows // clips
    half = 2 * length
    video = 4 * length
    scale = 1.0 / math.sqrt(HD)
    exponent = scale * math.log2(math.e)
    seg_at = 4 * count * length

    fetches = []
    for b in range(count):
        cols = pl.ds((first + b) * HD, HD)
        for a, (source, target) in enumerate(((q_any, raw_q), (k_any, raw_k), (t_any, raw_t))):
            copy = pltpu.make_async_copy(source.at[:, cols], target.at[b], in_sems.at[3 * b + a])
            copy.start()
            fetches.append(copy)

    me = lax.axis_index("ctx")
    end = (me == 0) | (me == 3)

    @pl.when(end)
    def _():
        pick[...] = last[...]

    @pl.when(jnp.logical_not(end))
    def _():
        pick[...] = far[...]

    pieces = (own, near, skip, pick)
    lane = lax.broadcasted_iota(jnp.int32, (length, HD), 1)
    sub = lax.broadcasted_iota(jnp.int32, (HD, length), 0).astype(F32)
    tops = []
    for s, piece in enumerate(pieces):
        seg = piece[pl.ds(seg_at, SEG_ROWS), :].astype(F32)[0:1, :]
        tops.append(jnp.max(seg))
        onehot = jnp.where(jnp.broadcast_to(seg, (HD, length)) == sub, 1.0, 0.0).T
        rows = pl.ds(s * length, length)
        q_mask = jnp.where(lane == clips, 1.0, onehot).astype(BF16)
        k_mask = jnp.where(lane < clips, (onehot - 1.0) * FAR, 0.0).astype(BF16)
        for b in range(count):
            qx[b, rows, HD:] = q_mask
            kx[b, rows, HD:] = k_mask
    flipped = me >= 2
    middle = jnp.where(
        flipped, jnp.maximum(tops[2], tops[3]), jnp.maximum(tops[0], tops[1])
    ).astype(jnp.int32)

    pairs = []
    for k in range(clips + 1):
        second = k > middle
        clip = jnp.where(second, k - 1, k)
        here = second == flipped
        at = pl.multiple_of(jnp.where(here, 0, half), half)
        pairs.append((clip, here, pl.ds(at, half)))

    def split_sum(x):
        return jnp.sum(x.reshape(x.shape[0] // 8, 8, x.shape[1]), axis=0)

    mine = slice(0, length)
    stores = []
    state = [{} for _ in range(count)]

    def columns(b):
        return pl.ds((first + b) * HD, HD)

    def put(source, target, b):
        copy = pltpu.make_async_copy(source, target.at[:, columns(b)], out_sems.at[len(stores)])
        copy.start()
        stores.append(copy)

    def text_at(b, clip):
        keys = pl.ds(pl.multiple_of((first + b) * text_rows + clip * per_clip, per_clip), per_clip)
        return keys, pl.ds(pl.multiple_of(clip * per_clip, per_clip), per_clip)

    def place(b):
        for s, piece in enumerate(pieces):
            rows = pl.ds(s * length, length)
            for a, ref in enumerate((qx, kx, vx, gx)):
                ref[b, rows, :HD] = piece[pl.ds((4 * b + a) * length, length), :]

    def video_scores(b):
        norm = [jnp.zeros((8, half), F32)] * 2
        mean = [jnp.zeros((8, half), F32)] * 2
        for j in range(2):
            for i in range(2):
                keys, rows = pl.ds(j * half, half), pl.ds(i * half, half)
                e = jnp.exp2(dot(kx[b, keys, :], qx[b, rows, :], (1, 1)) * exponent)
                dp = dot(vx[b, keys, :], gx[b, rows, :], (1, 1))
                norm[i] = norm[i] + split_sum(e)
                mean[i] = mean[i] + split_sum(e * dp)
                if j == 0:
                    e_row[b, :, rows] = e[mine, :].astype(BF16)
                    d_row[b, :, rows] = dp[mine, :]
                if i == 0:
                    e_col[b, keys, :] = e[:, mine].astype(BF16)
                    d_col[b, keys, :] = dp[:, mine]
        state[b].update(norm=norm, mean=mean)

    def text_scores(b, k):
        clip, here, rows = pairs[k]
        keys, vals = text_at(b, clip)
        e = jnp.exp2(dot(kt[keys, :], qx[b, rows, :], (1, 1)) * exponent)
        dp = dot(vt[vals, columns(b)], gx[b, rows, :], (1, 1))
        e_text[b, k] = e.astype(BF16)
        d_text[b, k] = dp
        for name, part in (("norm", split_sum(e)), ("mean", split_sum(e * dp))):
            sums = state[b][name]
            sums[0] = sums[0] + jnp.where(here, part, 0.0)
            sums[1] = sums[1] + jnp.where(here, 0.0, part)

    def close_sums(b):
        inv = [1.0 / jnp.sum(x, axis=0, keepdims=True) for x in state[b]["norm"]]
        inner = [jnp.sum(x, axis=0, keepdims=True) * y for x, y in zip(state[b]["mean"], inv)]
        for s in range(4):
            part = inv[s // 2][:, (s % 2) * length : (s % 2 + 1) * length]
            turned = jnp.broadcast_to(part, (HD, length)).T
            if s == 0:
                state[b]["turned"] = turned
            rows = pl.ds(s * length, length)
            qs[b, rows, :] = (qx[b, rows, :HD].astype(F32) * (turned * scale)).astype(BF16)
            gs[b, rows, :] = (gx[b, rows, :].astype(F32) * turned).astype(BF16)
        state[b].update(
            inner=inner, att=jnp.zeros((length, HD), F32), dq=jnp.zeros((length, HD), F32), before=None
        )

    def text_grads(b, k):
        me_b = state[b]
        clip, here, rows = pairs[k]
        keys, vals = text_at(b, clip)
        eb = e_text[b, k]
        away = jnp.where(here, me_b["inner"][0], me_b["inner"][1])
        ds = (eb.astype(F32) * (d_text[b, k] - away)).astype(BF16)
        dk = dot(ds, qs[b, rows, :], (1, 0))
        dv = dot(eb, gs[b, rows, :], (1, 0))
        me_b["att"] += jnp.where(here, dot(eb[:, mine], vt[vals, columns(b)], (0, 0)), 0.0)
        me_b["dq"] += jnp.where(here, dot(ds[:, mine], kt[keys, :HD], (0, 0)), 0.0)
        if k:
            c = k - 1
            low, high = c <= middle, c >= middle
            to = pl.ds(c * per_clip, per_clip)
            total = jnp.where(low, me_b["before"][0], 0.0) + jnp.where(high, dk, 0.0)
            x = raw_t[b, to, :].astype(F32)
            inverse = inv_t[pl.ds((first + b) * text_rows + c * per_clip, per_clip), :]
            along = jnp.sum(total * x, axis=-1, keepdims=True)
            staged_text[b, 0, to, :] = inverse * (
                total - x * (along * (inverse * inverse * (1.0 / HD)))
            )
            staged_text[b, 1, to, :] = jnp.where(low, me_b["before"][1], 0.0) + jnp.where(high, dv, 0.0)
        me_b["before"] = (dk, dv)

    def put_text(b):
        put(staged_text.at[b, 0], gtk, b)
        put(staged_text.at[b, 1], gtv, b)

    def video_grads(b):
        me_b = state[b]
        eb = e_row[b]
        inner_all = jnp.concatenate(me_b["inner"], axis=1)
        ds = (eb.astype(F32) * (d_row[b] - inner_all)).astype(BF16)
        dk = dot(ds, qs[b], (1, 0))
        dv = dot(eb, gs[b], (1, 0))
        eb = e_col[b]
        ds = (eb.astype(F32) * (d_col[b] - me_b["inner"][0][:, mine])).astype(BF16)
        att = me_b["att"] + dot(eb, vx[b], (0, 0))
        dq = me_b["dq"] + dot(ds, kx[b, :, :HD], (0, 0))
        turned = me_b["turned"]
        staged[b, 0] = (att * turned).astype(BF16)
        staged[b, 1] = norm_back(raw_q[b].astype(F32), dq * (turned * scale)).astype(BF16)
        staged[b, 2] = norm_back(raw_k[b].astype(F32), dk).astype(BF16)
        staged[b, 3] = dv.astype(BF16)

    def put_rows(b):
        for a, target in enumerate((out, gq, gk, gv)):
            put(staged.at[b, a], target, b)

    for b in range(count):
        place(b)
        video_scores(b)
        for k in range(clips + 1):
            text_scores(b, k)
        close_sums(b)
        for a in range(3):
            fetches[3 * b + a].wait()
        for k in range(clips + 1):
            text_grads(b, k)
        video_grads(b)
        put_text(b)
        put_rows(b)
    for copy in stores:
        copy.wait()


def attend_line(chunk, clips, pieces, text, queries, keys, text_keys, before):
    first, count = chunk
    length, width = queries.shape
    text_rows = text_keys.shape[0]
    per_clip = text_rows // clips
    half, video = 2 * length, 4 * length
    anywhere = pl.BlockSpec(memory_space=pl.ANY)
    remote = pl.BlockSpec(memory_space=pltpu.HBM)
    held = pl.BlockSpec(memory_space=pltpu.VMEM)
    out_rows = [length] * 4 + [text_rows] * 2
    out_types = [BF16] * 4 + [F32] * 2
    operands = [*pieces, *text, queries, keys, text_keys, *before]
    base = len(operands) - len(before)
    work = count * video * (video + text_rows)
    return pl.pallas_call(
        functools.partial(line_kernel, first, count, clips),
        in_specs=[held] * 8 + [remote] * 3 + [remote] * len(before),
        out_specs=[remote] * 6,
        out_shape=[
            jax.ShapeDtypeStruct((rows, width), dtype) for rows, dtype in zip(out_rows, out_types)
        ],
        scratch_shapes=[
            pltpu.VMEM((4 * count * length + SEG_ROWS, HD), BF16),
            pltpu.VMEM((count, video, 2 * HD), BF16),
            pltpu.VMEM((count, video, 2 * HD), BF16),
            pltpu.VMEM((count, video, HD), BF16),
            pltpu.VMEM((count, video, HD), BF16),
            pltpu.VMEM((count, video, HD), BF16),
            pltpu.VMEM((count, video, HD), BF16),
            pltpu.VMEM((count, length, video), BF16),
            pltpu.VMEM((count, video, length), BF16),
            pltpu.VMEM((count, clips + 1, per_clip, half), BF16),
            pltpu.VMEM((count, length, video), F32),
            pltpu.VMEM((count, video, length), F32),
            pltpu.VMEM((count, clips + 1, per_clip, half), F32),
            pltpu.VMEM((count, length, HD), BF16),
            pltpu.VMEM((count, length, HD), BF16),
            pltpu.VMEM((count, text_rows, HD), BF16),
            pltpu.VMEM((count, 4, length, HD), BF16),
            pltpu.VMEM((count, 2, text_rows, HD), F32),
            pltpu.SemaphoreType.DMA((3 * count,)),
            pltpu.SemaphoreType.DMA((6 * count,)),
        ],
        input_output_aliases={base + i: i for i in range(len(before))},
        compiler_params=pltpu.CompilerParams(vmem_limit_bytes=16 * 1024 * 1024),
        cost_estimate=pl.CostEstimate(
            flops=12 * work * HD, bytes_accessed=count * 2 * 1024 * 1024, transcendentals=work
        ),
        name="attend_line",
    )(*operands)


def shards(n, queries, keys, values, text_keys, text_values, segment, text_len, grad_out):
    heads = queries.shape[1] // HD
    half = max(heads // 2, 1)
    chunks = [(first, half) for first in range(0, heads, half)]
    payloads = pack(queries, keys, values, grad_out, segment, chunks)

    def send(x, pairs):
        return lax.ppermute(x, "ctx", pairs)

    if n == 4:
        outer = [(0, 1), (1, 0), (2, 3), (3, 2)]
        across = [(0, 2), (2, 0), (1, 3), (3, 1)]
        middle = [(1, 2), (2, 1)]
        outward = [(1, 0), (2, 3)]
        text = prepare_text(text_len, text_keys, text_values)

        def after(x, *others):
            return lax.optimization_barrier((x, *others))[0]

        a, b = payloads
        skip_a = send(a, across)
        near_a = send(after(a, *text), outer)
        skip_b = send(after(b, *text), across)
        near_b = send(b, outer)
        far_a = send(a, middle)
        far_b = send(after(b, near_b), middle)
        last_a = send(after(skip_a, near_b, *text), outward)
        last_b = send(skip_b, outward)
        pieces = [(a, near_a, skip_a, far_a, last_a), (b, near_b, skip_b, far_b, last_b)]
        outs = ()
        for chunk, piece in zip(chunks, pieces):
            outs = attend_line(
                chunk, text_len.shape[0], piece, text, queries, keys, text_keys, outs
            )
        return tuple(outs)
    outs = ()
    for chunk, x in zip(chunks, payloads):
        gathered = lax.all_gather(x, "ctx", axis=0)
        outs = attend(
            n, chunk, text_len, gathered, queries, keys, text_keys, text_values, outs
        )
    return tuple(outs)


def solution(mesh):
    rows = P(("groups", "ctx"), ("mp", "sec"))
    text = P("groups", ("mp", "sec"))
    in_specs = (rows, rows, rows, text, text, P(("groups", "ctx")), P("groups"), rows)
    out_specs = (rows, rows, rows, rows, text, text)
    return jax.shard_map(
        functools.partial(shards, mesh.shape["ctx"]),
        mesh=mesh,
        in_specs=in_specs,
        out_specs=out_specs,
        check_vma=False,
    )
```

```python
import functools
import math

import jax
import jax.numpy as jnp
from jax import lax
from jax.experimental import pallas as pl
from jax.experimental.pallas import tpu as pltpu
from jax.sharding import PartitionSpec as P

HD = 128
SEG_ROWS = 16
FAR = 16384.0
KEY_BLOCK = 256
ROW_BLOCK = 512

epsilon = 1e-06

F32 = jnp.float32
BF16 = jnp.bfloat16


def inverse_rms(x):
    return lax.rsqrt(jnp.mean(x * x, axis=-1, keepdims=True) + epsilon)


def norm_back(x, upstream):
    inverse = inverse_rms(x)
    inner = jnp.sum(upstream * x, axis=-1, keepdims=True) * (1.0 / HD)
    return upstream * inverse - x * (inner * inverse * inverse * inverse)


def dot(a, b, contract):
    return lax.dot_general(a, b, ((contract[:1], contract[1:]), ((), ())), preferred_element_type=F32)


def pack_kernel(chunks, q_ref, k_ref, v_ref, g_ref, seg_ref, *outs):
    length = q_ref.shape[0]
    for (first, count), out in zip(chunks, outs):
        for b in range(count):
            cols = pl.ds((first + b) * HD, HD)
            for a, ref in enumerate((q_ref, k_ref)):
                x = ref[:, cols].astype(F32)
                out[pl.ds((4 * b + a) * length, length), :] = (x * inverse_rms(x)).astype(BF16)
            for a, ref in enumerate((v_ref, g_ref)):
                out[pl.ds((4 * b + 2 + a) * length, length), :] = ref[:, cols]
        seg = seg_ref[...].astype(F32).astype(BF16)
        out[pl.ds(4 * count * length, SEG_ROWS), :] = jnp.broadcast_to(seg, (SEG_ROWS, length))


def pack(queries, keys, values, grad_out, segment, chunks):
    length = queries.shape[0]
    return pl.pallas_call(
        functools.partial(pack_kernel, chunks),
        out_shape=[
            jax.ShapeDtypeStruct((4 * count * length + SEG_ROWS, HD), BF16) for _, count in chunks
        ],
        name="pack",
    )(queries, keys, values, grad_out, segment.reshape(1, length))


def attend_kernel(n, length, count, *refs):
    refs = list(refs)
    len_ref = refs.pop(0)
    gathered = refs.pop(0)
    q_raw, k_raw, tk_ref, tv_ref = refs[:4]
    out_ref, gq_ref, gk_ref, gv_ref, gtk_ref, gtv_ref = refs[-18:-12]
    held, qx, kx, vx, gx, e_ref, dp_ref, dk_ref, dv_ref, dq_ref, att_ref, sems = refs[-12:]
    text_rows = tk_ref.shape[0]
    clips = len_ref.shape[0]
    per_clip = text_rows // clips
    video = n * length
    total = video + text_rows
    head = pl.program_id(0)
    rows_of = min(video, ROW_BLOCK)
    row_blocks = video // rows_of
    scale = 1.0 / math.sqrt(HD)
    exponent = scale * math.log2(math.e)
    seg_at = 4 * count * length

    @pl.when(head == 0)
    def _():
        me = lax.axis_index("ctx")
        def fetch(s, _):
            source = lax.rem(me + s, n)
            copy = pltpu.make_async_copy(gathered.at[source], held.at[s], sems.at[0])
            copy.start()
            copy.wait()
            return 0

        lax.fori_loop(0, n, fetch, 0)

        lane = lax.broadcasted_iota(jnp.int32, (length, HD), 1)
        sub = lax.broadcasted_iota(jnp.int32, (HD, length), 0).astype(F32)

        def mask_rows(s, _):
            seg = held[s, pl.ds(seg_at, SEG_ROWS), :].astype(F32)[0:1, :]
            onehot = jnp.where(jnp.broadcast_to(seg, (HD, length)) == sub, 1.0, 0.0).T
            rows = pl.ds(pl.multiple_of(s * length, length), length)
            qx[rows, HD:] = jnp.where(lane == clips, 1.0, onehot).astype(BF16)
            kx[rows, HD:] = jnp.where(lane < clips, (onehot - 1.0) * FAR, 0.0).astype(BF16)
            return 0

        lax.fori_loop(0, n, mask_rows, 0, unroll=n <= 4)
        lane = lax.broadcasted_iota(jnp.int32, (per_clip, HD), 1)
        place = lax.broadcasted_iota(jnp.int32, (per_clip, HD), 0)
        for c in range(clips):
            other = jnp.where((lane < clips) & (lane != c), -FAR, 0.0)
            dead = jnp.where((lane == clips) & (place >= len_ref[c]), -FAR, 0.0)
            kx[pl.ds(video + c * per_clip, per_clip), HD:] = (other + dead).astype(BF16)

    def place_rows(s, _):
        rows = pl.ds(pl.multiple_of(s * length, length), length)
        for a, (ref, cols) in enumerate(((qx, pl.ds(0, HD)), (kx, pl.ds(0, HD)), (vx, pl.ds(0, HD)), (gx, pl.ds(0, HD)))):
            at = pl.multiple_of((4 * head + a) * length, length)
            ref[rows, cols] = held[s, pl.ds(at, length), :]
        return 0

    lax.fori_loop(0, n, place_rows, 0, unroll=n <= 4)
    text = tk_ref[...].astype(F32)
    kx[pl.ds(video, text_rows), :HD] = (text * inverse_rms(text)).astype(BF16)
    vx[pl.ds(video, text_rows), :] = tv_ref[...]

    def rows_step(rb, first):
        rows = pl.ds(pl.multiple_of(rb * rows_of, rows_of), rows_of)
        q_all = qx[rows, :]
        q_here = qx[rows, :HD]
        g_here = gx[rows, :]

        def score(kb, sums):
            at = pl.ds(pl.multiple_of(kb * KEY_BLOCK, KEY_BLOCK), KEY_BLOCK)
            e = jnp.exp2(dot(kx[at, :], q_all, (1, 1)) * exponent)
            dp = dot(vx[at, :], g_here, (1, 1))
            e_ref[at, :] = e
            dp_ref[at, :] = dp
            shape = (KEY_BLOCK // 8, 8, rows_of)
            return (
                sums[0] + jnp.sum(e.reshape(shape), axis=0),
                sums[1] + jnp.sum((e * dp).reshape(shape), axis=0),
            )

        blocks = total // KEY_BLOCK
        zero = jnp.zeros((8, rows_of), F32)
        sums = lax.fori_loop(0, blocks, score, (zero, zero), unroll=blocks <= 8)
        inv = 1.0 / jnp.sum(sums[0], axis=0, keepdims=True)
        inner = jnp.sum(sums[1], axis=0, keepdims=True) * inv

        def add(ref, at, value):
            if row_blocks == 1:
                ref[at, :] = value
            else:
                ref[at, :] = jnp.where(rb == 0, value, ref[at, :] + value)

        def terms(at, cols):
            p = e_ref[at, cols] * inv[:, cols]
            ds = p * (dp_ref[at, cols] - inner[:, cols])
            return p.astype(BF16), ds.astype(BF16)

        everything = slice(0, rows_of)
        mine = slice(0, length)

        def query_side(at, p, ds, start):
            att = dot(p, vx[at, :], (0, 0))
            dq = dot(ds, kx[at, :HD], (0, 0))
            if start:
                att_ref[...] = att
                dq_ref[...] = dq
            else:
                att_ref[...] += att
                dq_ref[...] += dq

        def own_rows(at, p, ds, start=False):
            if row_blocks == 1:
                query_side(at, p[:, mine], ds[:, mine], start)
            else:

                @pl.when(rb == 0)
                def _():
                    query_side(at, p[:, mine], ds[:, mine], start)

        own = pl.ds(0, length)
        p, ds = terms(own, everything)
        add(dk_ref, own, dot(ds, q_here, (1, 0)))
        add(dv_ref, own, dot(p, g_here, (1, 0)))
        own_rows(own, p, ds, True)

        def others():
            def other(s, _):
                at = pl.ds(pl.multiple_of(s * length, length), length)
                p, ds = terms(at, mine)
                query_side(at, p, ds, False)
                return 0

            lax.fori_loop(1, n, other, 0, unroll=n <= 4)

        if row_blocks == 1:
            others()
        else:
            pl.when(rb == 0)(others)
        for c in range(text_rows // KEY_BLOCK):
            at = pl.ds(video + c * KEY_BLOCK, KEY_BLOCK)
            to = pl.ds(c * KEY_BLOCK, KEY_BLOCK)
            p, ds = terms(at, everything)
            add(gtk_ref, to, dot(ds, q_here, (1, 0)))
            add(gtv_ref, to, dot(p, g_here, (1, 0)))
            own_rows(at, p, ds)

    if row_blocks == 1:
        rows_step(0, True)
    else:

        def step(rb, _):
            rows_step(rb, False)
            return 0

        lax.fori_loop(0, row_blocks, step, 0)

    out_ref[...] = att_ref[...].astype(BF16)
    gq_ref[...] = norm_back(q_raw[...].astype(F32), dq_ref[...] * scale).astype(BF16)
    gk_ref[...] = norm_back(k_raw[...].astype(F32), dk_ref[...] * scale).astype(BF16)
    gv_ref[...] = dv_ref[...].astype(BF16)
    gtk_ref[...] = norm_back(tk_ref[...].astype(F32), gtk_ref[...] * scale)


def attend(n, chunk, text_len, gathered, queries, keys, text_keys, text_values, before):
    first, count = chunk
    length, width = queries.shape
    text_rows = text_keys.shape[0]
    video = n * length
    total = video + text_rows
    rows_of = min(video, ROW_BLOCK)
    anywhere = pl.BlockSpec(memory_space=pl.ANY)

    def column(rows):
        return pl.BlockSpec((rows, HD), lambda h: (0, first + h))

    in_specs = (
        [pl.BlockSpec(memory_space=pltpu.SMEM)]
        + [anywhere]
        + [column(length)] * 2
        + [column(text_rows)] * 2
        + [anywhere] * len(before)
    )
    out_rows = [length] * 4 + [text_rows] * 2
    out_types = [BF16] * 4 + [F32] * 2
    operands = [text_len, gathered, queries, keys, text_keys, text_values, *before]
    base = len(operands) - len(before)
    pairs = count * total * rows_of * (video // rows_of)
    return pl.pallas_call(
        functools.partial(attend_kernel, n, length, count),
        grid=(count,),
        in_specs=in_specs,
        out_specs=[column(rows) for rows in out_rows],
        out_shape=[
            jax.ShapeDtypeStruct((rows, width), dtype) for rows, dtype in zip(out_rows, out_types)
        ],
        scratch_shapes=[
            pltpu.VMEM((n, 4 * count * length + SEG_ROWS, HD), BF16),
            pltpu.VMEM((video, 2 * HD), BF16),
            pltpu.VMEM((total, 2 * HD), BF16),
            pltpu.VMEM((total, HD), BF16),
            pltpu.VMEM((video, HD), BF16),
            pltpu.VMEM((total, rows_of), F32),
            pltpu.VMEM((total, rows_of), F32),
            pltpu.VMEM((length, HD), F32),
            pltpu.VMEM((length, HD), F32),
            pltpu.VMEM((length, HD), F32),
            pltpu.VMEM((length, HD), F32),
            pltpu.SemaphoreType.DMA((1,)),
        ],
        input_output_aliases={base + i: i for i in range(len(before))},
        compiler_params=pltpu.CompilerParams(vmem_limit_bytes=56 * 1024 * 1024),
        cost_estimate=pl.CostEstimate(
            flops=12 * pairs * HD, bytes_accessed=count * 3 * 1024 * 1024, transcendentals=pairs
        ),
        name="attend",
    )(*operands)


def text_kernel(len_ref, tk_ref, tv_ref, kt_ref, vt_ref, inv_ref):
    text_rows, width = tk_ref.shape
    clips = len_ref.shape[0]
    per_clip = text_rows // clips
    lane = lax.broadcasted_iota(jnp.int32, (per_clip, HD), 1)
    place = lax.broadcasted_iota(jnp.int32, (per_clip, HD), 0)
    for c in range(clips):
        other = jnp.where((lane < clips) & (lane != c), -FAR, 0.0)
        dead = jnp.where((lane == clips) & (place >= len_ref[c]), -FAR, 0.0)
        mask = (other + dead).astype(BF16)
        rows = pl.ds(c * per_clip, per_clip)
        for h in range(width // HD):
            to = pl.ds(h * text_rows + c * per_clip, per_clip)
            x = tk_ref[rows, pl.ds(h * HD, HD)].astype(F32)
            inverse = inverse_rms(x)
            kt_ref[to, :HD] = (x * inverse).astype(BF16)
            kt_ref[to, HD:] = mask
            inv_ref[to, :] = jnp.broadcast_to(inverse, (per_clip, HD))
    vt_ref[...] = tv_ref[...]


def prepare_text(text_len, text_keys, text_values):
    text_rows, width = text_keys.shape
    whole = pl.BlockSpec(memory_space=pltpu.VMEM)
    return pl.pallas_call(
        text_kernel,
        in_specs=[pl.BlockSpec(memory_space=pltpu.SMEM), whole, whole],
        out_specs=[whole, whole, whole],
        out_shape=[
            jax.ShapeDtypeStruct((width // HD * text_rows, 2 * HD), BF16),
            jax.ShapeDtypeStruct((text_rows, width), BF16),
            jax.ShapeDtypeStruct((width // HD * text_rows, HD), F32),
        ],
        compiler_params=pltpu.CompilerParams(vmem_limit_bytes=16 * 1024 * 1024),
        cost_estimate=pl.CostEstimate(
            flops=8 * text_rows * width, bytes_accessed=6 * text_rows * width, transcendentals=0
        ),
        name="prepare_text",
    )(text_len, text_keys, text_values)


def line_kernel(first, count, clips, *refs):
    own, near, skip, far, last, kt, vt, inv_t, q_any, k_any, t_any = refs[:11]
    out, gq, gk, gv, gtk, gtv = refs[-26:-20]
    (pick, qx, kx, vx, gx, qs, gs, e_row, e_col, e_text, d_row, d_col, d_text) = refs[-20:-7]
    raw_q, raw_k, raw_t, staged, staged_text, in_sems, out_sems = refs[-7:]
    length = raw_q.shape[1]
    text_rows = vt.shape[0]
    per_clip = text_rows // clips
    half = 2 * length
    video = 4 * length
    scale = 1.0 / math.sqrt(HD)
    exponent = scale * math.log2(math.e)
    seg_at = 4 * count * length

    fetches = []
    for b in range(count):
        cols = pl.ds((first + b) * HD, HD)
        for a, (source, target) in enumerate(((q_any, raw_q), (k_any, raw_k), (t_any, raw_t))):
            copy = pltpu.make_async_copy(source.at[:, cols], target.at[b], in_sems.at[3 * b + a])
            copy.start()
            fetches.append(copy)

    me = lax.axis_index("ctx")
    end = (me == 0) | (me == 3)

    @pl.when(end)
    def _():
        pick[...] = last[...]

    @pl.when(jnp.logical_not(end))
    def _():
        pick[...] = far[...]

    pieces = (own, near, skip, pick)
    lane = lax.broadcasted_iota(jnp.int32, (length, HD), 1)
    sub = lax.broadcasted_iota(jnp.int32, (HD, length), 0).astype(F32)
    tops = []
    for s, piece in enumerate(pieces):
        seg = piece[pl.ds(seg_at, SEG_ROWS), :].astype(F32)[0:1, :]
        tops.append(jnp.max(seg))
        onehot = jnp.where(jnp.broadcast_to(seg, (HD, length)) == sub, 1.0, 0.0).T
        rows = pl.ds(s * length, length)
        q_mask = jnp.where(lane == clips, 1.0, onehot).astype(BF16)
        k_mask = jnp.where(lane < clips, (onehot - 1.0) * FAR, 0.0).astype(BF16)
        for b in range(count):
            qx[b, rows, HD:] = q_mask
            kx[b, rows, HD:] = k_mask
    flipped = me >= 2
    middle = jnp.where(
        flipped, jnp.maximum(tops[2], tops[3]), jnp.maximum(tops[0], tops[1])
    ).astype(jnp.int32)

    pairs = []
    for k in range(clips + 1):
        second = k > middle
        clip = jnp.where(second, k - 1, k)
        here = second == flipped
        at = pl.multiple_of(jnp.where(here, 0, half), half)
        pairs.append((clip, here, pl.ds(at, half)))

    def split_sum(x):
        return jnp.sum(x.reshape(x.shape[0] // 8, 8, x.shape[1]), axis=0)

    mine = slice(0, length)
    stores = []
    state = [{} for _ in range(count)]

    def columns(b):
        return pl.ds((first + b) * HD, HD)

    def put(source, target, b):
        copy = pltpu.make_async_copy(source, target.at[:, columns(b)], out_sems.at[len(stores)])
        copy.start()
        stores.append(copy)

    def text_at(b, clip):
        keys = pl.ds(pl.multiple_of((first + b) * text_rows + clip * per_clip, per_clip), per_clip)
        return keys, pl.ds(pl.multiple_of(clip * per_clip, per_clip), per_clip)

    def place(b):
        for s, piece in enumerate(pieces):
            rows = pl.ds(s * length, length)
            for a, ref in enumerate((qx, kx, vx, gx)):
                ref[b, rows, :HD] = piece[pl.ds((4 * b + a) * length, length), :]

    def video_scores(b):
        norm = [jnp.zeros((8, half), F32)] * 2
        mean = [jnp.zeros((8, half), F32)] * 2
        for j in range(2):
            for i in range(2):
                keys, rows = pl.ds(j * half, half), pl.ds(i * half, half)
                e = jnp.exp2(dot(kx[b, keys, :], qx[b, rows, :], (1, 1)) * exponent)
                dp = dot(vx[b, keys, :], gx[b, rows, :], (1, 1))
                norm[i] = norm[i] + split_sum(e)
                mean[i] = mean[i] + split_sum(e * dp)
                if j == 0:
                    e_row[b, :, rows] = e[mine, :].astype(BF16)
                    d_row[b, :, rows] = dp[mine, :]
                if i == 0:
                    e_col[b, keys, :] = e[:, mine].astype(BF16)
                    d_col[b, keys, :] = dp[:, mine]
        state[b].update(norm=norm, mean=mean)

    def text_scores(b, k):
        clip, here, rows = pairs[k]
        keys, vals = text_at(b, clip)
        e = jnp.exp2(dot(kt[keys, :], qx[b, rows, :], (1, 1)) * exponent)
        dp = dot(vt[vals, columns(b)], gx[b, rows, :], (1, 1))
        e_text[b, k] = e.astype(BF16)
        d_text[b, k] = dp
        for name, part in (("norm", split_sum(e)), ("mean", split_sum(e * dp))):
            sums = state[b][name]
            sums[0] = sums[0] + jnp.where(here, part, 0.0)
            sums[1] = sums[1] + jnp.where(here, 0.0, part)

    def close_sums(b):
        inv = [1.0 / jnp.sum(x, axis=0, keepdims=True) for x in state[b]["norm"]]
        inner = [jnp.sum(x, axis=0, keepdims=True) * y for x, y in zip(state[b]["mean"], inv)]
        for s in range(4):
            part = inv[s // 2][:, (s % 2) * length : (s % 2 + 1) * length]
            turned = jnp.broadcast_to(part, (HD, length)).T
            if s == 0:
                state[b]["turned"] = turned
            rows = pl.ds(s * length, length)
            qs[b, rows, :] = (qx[b, rows, :HD].astype(F32) * (turned * scale)).astype(BF16)
            gs[b, rows, :] = (gx[b, rows, :].astype(F32) * turned).astype(BF16)
        state[b].update(
            inner=inner, att=jnp.zeros((length, HD), F32), dq=jnp.zeros((length, HD), F32), before=None
        )

    def text_grads(b, k):
        me_b = state[b]
        clip, here, rows = pairs[k]
        keys, vals = text_at(b, clip)
        eb = e_text[b, k]
        away = jnp.where(here, me_b["inner"][0], me_b["inner"][1])
        ds = (eb.astype(F32) * (d_text[b, k] - away)).astype(BF16)
        dk = dot(ds, qs[b, rows, :], (1, 0))
        dv = dot(eb, gs[b, rows, :], (1, 0))
        me_b["att"] += jnp.where(here, dot(eb[:, mine], vt[vals, columns(b)], (0, 0)), 0.0)
        me_b["dq"] += jnp.where(here, dot(ds[:, mine], kt[keys, :HD], (0, 0)), 0.0)
        if k:
            c = k - 1
            low, high = c <= middle, c >= middle
            to = pl.ds(c * per_clip, per_clip)
            total = jnp.where(low, me_b["before"][0], 0.0) + jnp.where(high, dk, 0.0)
            x = raw_t[b, to, :].astype(F32)
            inverse = inv_t[pl.ds((first + b) * text_rows + c * per_clip, per_clip), :]
            along = jnp.sum(total * x, axis=-1, keepdims=True)
            staged_text[b, 0, to, :] = inverse * (
                total - x * (along * (inverse * inverse * (1.0 / HD)))
            )
            staged_text[b, 1, to, :] = jnp.where(low, me_b["before"][1], 0.0) + jnp.where(high, dv, 0.0)
        me_b["before"] = (dk, dv)

    def put_text(b):
        put(staged_text.at[b, 0], gtk, b)
        put(staged_text.at[b, 1], gtv, b)

    def video_grads(b):
        me_b = state[b]
        eb = e_row[b]
        inner_all = jnp.concatenate(me_b["inner"], axis=1)
        ds = (eb.astype(F32) * (d_row[b] - inner_all)).astype(BF16)
        dk = dot(ds, qs[b], (1, 0))
        dv = dot(eb, gs[b], (1, 0))
        eb = e_col[b]
        ds = (eb.astype(F32) * (d_col[b] - me_b["inner"][0][:, mine])).astype(BF16)
        att = me_b["att"] + dot(eb, vx[b], (0, 0))
        dq = me_b["dq"] + dot(ds, kx[b, :, :HD], (0, 0))
        turned = me_b["turned"]
        staged[b, 0] = (att * turned).astype(BF16)
        staged[b, 1] = norm_back(raw_q[b].astype(F32), dq * (turned * scale)).astype(BF16)
        staged[b, 2] = norm_back(raw_k[b].astype(F32), dk).astype(BF16)
        staged[b, 3] = dv.astype(BF16)

    def put_rows(b):
        for a, target in enumerate((out, gq, gk, gv)):
            put(staged.at[b, a], target, b)

    for b in range(count):
        place(b)
        video_scores(b)
        for k in range(clips + 1):
            text_scores(b, k)
        close_sums(b)
        for a in range(3):
            fetches[3 * b + a].wait()
        for k in range(clips + 1):
            text_grads(b, k)
        video_grads(b)
        put_text(b)
        put_rows(b)
    for copy in stores:
        copy.wait()


def attend_line(chunk, clips, pieces, text, queries, keys, text_keys, before):
    first, count = chunk
    length, width = queries.shape
    text_rows = text_keys.shape[0]
    per_clip = text_rows // clips
    half, video = 2 * length, 4 * length
    anywhere = pl.BlockSpec(memory_space=pl.ANY)
    remote = pl.BlockSpec(memory_space=pltpu.HBM)
    held = pl.BlockSpec(memory_space=pltpu.VMEM)
    out_rows = [length] * 4 + [text_rows] * 2
    out_types = [BF16] * 4 + [F32] * 2
    operands = [*pieces, *text, queries, keys, text_keys, *before]
    base = len(operands) - len(before)
    work = count * video * (video + text_rows)
    return pl.pallas_call(
        functools.partial(line_kernel, first, count, clips),
        in_specs=[held] * 8 + [remote] * 3 + [remote] * len(before),
        out_specs=[remote] * 6,
        out_shape=[
            jax.ShapeDtypeStruct((rows, width), dtype) for rows, dtype in zip(out_rows, out_types)
        ],
        scratch_shapes=[
            pltpu.VMEM((4 * count * length + SEG_ROWS, HD), BF16),
            pltpu.VMEM((count, video, 2 * HD), BF16),
            pltpu.VMEM((count, video, 2 * HD), BF16),
            pltpu.VMEM((count, video, HD), BF16),
            pltpu.VMEM((count, video, HD), BF16),
            pltpu.VMEM((count, video, HD), BF16),
            pltpu.VMEM((count, video, HD), BF16),
            pltpu.VMEM((count, length, video), BF16),
            pltpu.VMEM((count, video, length), BF16),
            pltpu.VMEM((count, clips + 1, per_clip, half), BF16),
            pltpu.VMEM((count, length, video), F32),
            pltpu.VMEM((count, video, length), F32),
            pltpu.VMEM((count, clips + 1, per_clip, half), F32),
            pltpu.VMEM((count, length, HD), BF16),
            pltpu.VMEM((count, length, HD), BF16),
            pltpu.VMEM((count, text_rows, HD), BF16),
            pltpu.VMEM((count, 4, length, HD), BF16),
            pltpu.VMEM((count, 2, text_rows, HD), F32),
            pltpu.SemaphoreType.DMA((3 * count,)),
            pltpu.SemaphoreType.DMA((6 * count,)),
        ],
        input_output_aliases={base + i: i for i in range(len(before))},
        compiler_params=pltpu.CompilerParams(vmem_limit_bytes=16 * 1024 * 1024),
        cost_estimate=pl.CostEstimate(
            flops=12 * work * HD, bytes_accessed=count * 2 * 1024 * 1024, transcendentals=work
        ),
        name="attend_line",
    )(*operands)


def shards(n, queries, keys, values, text_keys, text_values, segment, text_len, grad_out):
    heads = queries.shape[1] // HD
    half = max(heads // 2, 1)
    chunks = [(first, half) for first in range(0, heads, half)]
    payloads = pack(queries, keys, values, grad_out, segment, chunks)

    def send(x, pairs):
        return lax.ppermute(x, "ctx", pairs)

    if n == 4:
        outer = [(0, 1), (1, 0), (2, 3), (3, 2)]
        across = [(0, 2), (2, 0), (1, 3), (3, 1)]
        middle = [(1, 2), (2, 1)]
        outward = [(1, 0), (2, 3)]
        text = prepare_text(text_len, text_keys, text_values)

        def after(x, *others):
            return lax.optimization_barrier((x, *others))[0]

        a, b = payloads
        skip_a = send(a, across)
        near_b = send(b, outer)
        near_a = send(after(a, *text), outer)
        skip_b = send(after(b, *text), across)
        far_a = send(after(a, near_b), middle)
        far_b = send(after(b, near_b), middle)
        last_a = send(after(skip_a, near_b, *text), outward)
        last_b = send(skip_b, outward)
        pieces = [(a, near_a, skip_a, far_a, last_a), (b, near_b, skip_b, far_b, last_b)]
        outs = ()
        for chunk, piece in zip(chunks, pieces):
            outs = attend_line(
                chunk, text_len.shape[0], piece, text, queries, keys, text_keys, outs
            )
        return tuple(outs)
    outs = ()
    for chunk, x in zip(chunks, payloads):
        gathered = lax.all_gather(x, "ctx", axis=0)
        outs = attend(
            n, chunk, text_len, gathered, queries, keys, text_keys, text_values, outs
        )
    return tuple(outs)


def solution(mesh):
    rows = P(("groups", "ctx"), ("mp", "sec"))
    text = P("groups", ("mp", "sec"))
    in_specs = (rows, rows, rows, text, text, P(("groups", "ctx")), P("groups"), rows)
    out_specs = (rows, rows, rows, rows, text, text)
    return jax.shard_map(
        functools.partial(shards, mesh.shape["ctx"]),
        mesh=mesh,
        in_specs=in_specs,
        out_specs=out_specs,
        check_vma=False,
    )
```
